32 devices in a mesh: row: 4 (over y, core), col: 8 (over z, x).
Axes of the slice: x: 2, y: 2, z: 4, core: 2. Of those that a mesh axis runs over, the one named last changes fastest.
Arguments:
- features: bfloat16 [8192, 256], P(('col', 'row')), may hold values from -6 to 6
- adj_tiles: bfloat16 [4, 8, 16, 256, 256], P('row', 'col'), may hold values from -0.1875 to 0.1875
- tile_rows: int32 [4, 8, 16], P('row', 'col'), may hold values from 0 to 7, as said below
- tile_cols: int32 [4, 8, 16], P('row', 'col'), may hold values from 0 to 3, as said below
- tile_count: int32 [4, 8], P('row', 'col'), may hold values from 1 to 16, as said below
- weight: bfloat16 [256, 256], replicated, may hold values from -0.375 to 0.375
- grad_out: bfloat16 [8192, 256], P(('row', 'col')), may hold values from -6 to 6
Outputs:
- activation: bfloat16 [8192, 256], P(('row', 'col'))
- weight_grad: float32 [256, 256], replicated
- x_grad: bfloat16 [8192, 256], P(('col', 'row'))
The draws below stay inside these ranges and needn't reach their ends.
Inputs may be any that keep to these rules, and one draw needn't show every extreme that they name: On each grid block the 16 slots name distinct tile positions (tile_rows, tile_cols). `tile_cols`: paired with tile_rows slot by slot. `tile_count`: slots of a grid block at or beyond its count are ignored.
All inputs are finite; a program needn't handle non-finite values.
Results may differ from the reference program's by a relative error of at most 0.025.
Values may be sent and summed in bfloat16 or wider, within the bound.
A program may use at most 128 MiB of HBM per device.

```python
import math
import jax
import jax.numpy as jnp
from jax import lax

F = 256
TILE = 256
ROWS_DEV = 256
NODES = 8192
BR = 8
BC = 4
TILES_DEV = 16
N_ROW = 4
N_COL = 8


def tile_positions(key):
    position_total = BR * BC
    device_total = N_ROW * N_COL
    spots = jnp.arange(position_total, dtype=jnp.int32)

    def rank_one(subkey, device_id):
        scores = jax.random.randint(subkey, (position_total,), 0, 1 << 19) * position_total + spots
        forced = jnp.where(device_id == 0, position_total - 1, 0)
        scores = jnp.where((device_id < 2) & (spots == forced), -1, scores)
        return jnp.argsort(scores, stable=True)[:TILES_DEV].astype(jnp.int32)
    device_keys = jax.random.split(jax.random.fold_in(key, 11), device_total)
    chosen = jax.vmap(rank_one)(device_keys, jnp.arange(device_total, dtype=jnp.int32))
    return chosen.reshape(N_ROW, N_COL, TILES_DEV)


def draw_tile_rows(key, part):
    return tile_positions(key) // BC


def draw_tile_cols(key, part):
    return tile_positions(key) % BC


def draw_tile_count(key, part):
    device_total = N_ROW * N_COL
    subkeys = jax.random.split(jax.random.fold_in(key, 23), 4)
    factor_one = jax.random.randint(subkeys[0], (device_total,), 1, TILES_DEV + 1)
    factor_two = jax.random.randint(subkeys[1], (device_total,), 1, TILES_DEV + 1)
    counts = jnp.maximum(1, factor_one * factor_two // TILES_DEV)
    device_ids = jnp.arange(device_total, dtype=jnp.int32)
    busiest = jax.random.randint(subkeys[2], (), 0, device_total)
    lightest = (busiest + 1 + jax.random.randint(subkeys[3], (), 0, device_total - 1)) % device_total
    counts = jnp.where(device_ids == busiest, TILES_DEV, counts)
    counts = jnp.where(device_ids == lightest, 1, counts)
    return counts.reshape(N_ROW, N_COL).astype(jnp.int32)


def shard_levels(key, dims, pieces, low, largest):
    def one(dim, blocks):
        steps = jax.random.uniform(jax.random.fold_in(jax.random.fold_in(key, 6), dim), (blocks,), jnp.float32, low / len(pieces), largest / len(pieces))
        return jnp.repeat(jnp.exp(steps), dims[dim] // blocks).reshape((-1,) + (1,) * (len(dims) - dim - 1))

    level = one(*pieces[0])
    for cut in pieces[1:]:
        level = level * one(*cut)
    return level


def normal_values(own_key, dims, scale, reach, cuts=(), held_as=jnp.bfloat16):
    drawn = scale * jax.random.normal(own_key, dims, jnp.float32)
    if cuts:
        drawn = drawn * shard_levels(own_key, dims, cuts, -0.22, 0.18)
    return jnp.clip(drawn, -reach, reach).astype(held_as)


def setup_inputs(seed: int = 0) -> dict:
    streams_of = jax.random.split(jax.random.key(seed), 8)
    features = normal_values(streams_of[0], (NODES, F), 1.0, 6.0, ((0, 32),))
    adj_tiles = normal_values(streams_of[1], (N_ROW, N_COL, TILES_DEV, TILE, TILE), (max(1, TILES_DEV * TILE * TILE // (4 * ROWS_DEV))) ** -0.5, 0.1875, ((0, 4), (1, 8)))
    tile_rows = draw_tile_rows(jax.random.fold_in(streams_of[7], 71), 0)
    tile_cols = draw_tile_cols(jax.random.fold_in(streams_of[7], 71), 0)
    tile_count = draw_tile_count(jax.random.fold_in(streams_of[7], 71), 0)
    weight = normal_values(streams_of[5], (F, F), F ** -0.5, 0.375)
    grad_out = normal_values(streams_of[6], (NODES, F), 1.0, 6.0, ((0, 32),))
    return dict(features=features, adj_tiles=adj_tiles, tile_rows=tile_rows, tile_cols=tile_cols, tile_count=tile_count, weight=weight, grad_out=grad_out)


def reference(features, adj_tiles, tile_rows, tile_cols, tile_count, weight, grad_out):
    block_rows = BR * TILE
    block_cols = BC * TILE
    slot_ids = jnp.arange(TILES_DEV, dtype=jnp.int32)

    def forward_block(block_row):

        def over_cols(running, block_col):
            blocks = adj_tiles[block_row, block_col].astype(jnp.float32)
            row_ids = tile_rows[block_row, block_col]
            col_ids = tile_cols[block_row, block_col]
            active = (slot_ids < tile_count[block_row, block_col]).astype(jnp.float32)
            col_panel = lax.dynamic_slice_in_dim(features, (block_col * block_cols).astype(jnp.int32), block_cols, 0)
            col_panel = col_panel.reshape(BC, TILE, F).astype(jnp.float32)
            product = jnp.einsum('gij,gjf->gif', blocks, col_panel[col_ids]) * active[:, None, None]
            partial_sum = jnp.zeros((BR, TILE, F), jnp.float32).at[row_ids].add(product)
            rounded = lax.optimization_barrier(partial_sum.astype(jnp.bfloat16))
            return (running + rounded.astype(jnp.float32), None)
        running, _ = lax.scan(over_cols, jnp.zeros((BR, TILE, F), jnp.float32), jnp.arange(N_COL, dtype=jnp.int32))
        return running.astype(jnp.bfloat16)
    aggregated = lax.map(forward_block, jnp.arange(N_ROW, dtype=jnp.int32)).reshape(NODES, F)
    pre_act = jnp.dot(aggregated, weight, preferred_element_type=jnp.float32)
    gate_sig = jax.nn.sigmoid(pre_act)
    activation = (pre_act * gate_sig).astype(jnp.bfloat16)
    silu_slope = gate_sig * (1.0 + pre_act * (1.0 - gate_sig))
    act_grad = (grad_out.astype(jnp.float32) * silu_slope).astype(jnp.bfloat16)
    grad_scale = 1.0 / math.sqrt(NODES)
    weight_grad = lax.dot_general(aggregated, act_grad, (((0,), (0,)), ((), ())), preferred_element_type=jnp.float32) * grad_scale
    msg_grad = jnp.dot(act_grad, weight.T, preferred_element_type=jnp.float32).astype(jnp.bfloat16)

    def backward_block(block_col):

        def over_rows(running, block_row):
            blocks = adj_tiles[block_row, block_col].astype(jnp.float32)
            row_ids = tile_rows[block_row, block_col]
            col_ids = tile_cols[block_row, block_col]
            active = (slot_ids < tile_count[block_row, block_col]).astype(jnp.float32)
            row_panel = lax.dynamic_slice_in_dim(msg_grad, (block_row * block_rows).astype(jnp.int32), block_rows, 0)
            row_panel = row_panel.reshape(BR, TILE, F).astype(jnp.float32)
            product = jnp.einsum('gij,gif->gjf', blocks, row_panel[row_ids]) * active[:, None, None]
            partial_sum = jnp.zeros((BC, TILE, F), jnp.float32).at[col_ids].add(product)
            rounded = lax.optimization_barrier(partial_sum.astype(jnp.bfloat16))
            return (running + rounded.astype(jnp.float32), None)
        running, _ = lax.scan(over_rows, jnp.zeros((BC, TILE, F), jnp.float32), jnp.arange(N_ROW, dtype=jnp.int32))
        return running.astype(jnp.bfloat16)
    x_grad = lax.map(backward_block, jnp.arange(N_COL, dtype=jnp.int32)).reshape(NODES, F)
    return (activation, weight_grad, x_grad)
```

```python
import functools
import math

import jax
import jax.numpy as jnp
from jax import lax
from jax.experimental import pallas as pl
from jax.experimental.pallas import tpu as pltpu
from jax.sharding import PartitionSpec as P

MESH = pl.DeviceIdType.MESH
BF16 = jnp.bfloat16
F32 = jnp.float32


def dot(a, b):
    return jnp.dot(a, b, preferred_element_type=F32)


def kernel(
    R, C, S, T, F, scale,
    feat, adj, trow, tcol, tcnt, wt, gout,
    act_out, wg_out, xg_out,
    tiles, xs, wv, gv, pos, inv, accf,
    xsend, xrecv, zsend, zrecv, actv, mt, bacc,
    bsend, brecv, osend, orecv, xgv,
    wterm, wr1, wr2, wr3, wgv,
    loc, fs, fr, ps, pr, zs, zr, ms, mr, bs, br, os_, or_,
    w1s, w1r, w2s, w2r, w3s, w3r,
):
    r = lax.axis_index("row")
    c = lax.axis_index("col")
    Ro, Z = R // 2, C // 2
    yo, k = r // 2, r % 2
    z, x = c // 2, c % 2
    inner = yo * 2 + 1 - k
    xpeer = z * 2 + 1 - x
    H = T // C

    def remote(src, dst, ss, rs, row, col):
        return pltpu.make_async_remote_copy(
            src_ref=src, dst_ref=dst, send_sem=ss, recv_sem=rs,
            device_id={"row": row, "col": col}, device_id_type=MESH,
        )

    def arrived(dst, rs):
        pltpu.make_async_copy(dst, dst, rs).wait()

    c_feat = pltpu.make_async_copy(feat, xs.at[r], loc.at[0])
    c_feat.start()
    c_adj = pltpu.make_async_copy(adj.at[0, 0], tiles.at[pl.ds(0, S)], loc.at[1])
    c_adj.start()
    c_w = pltpu.make_async_copy(wt, wv, loc.at[2])
    c_w.start()
    c_g = pltpu.make_async_copy(gout, gv, loc.at[3])
    c_g.start()

    barrier = pltpu.get_barrier_semaphore()
    for o in range(1, R):
        pl.semaphore_signal(
            barrier, inc=1, device_id={"row": (r + o) % R, "col": c}, device_id_type=MESH)
    for o in range(1, C):
        pl.semaphore_signal(
            barrier, inc=1, device_id={"row": r, "col": (c + o) % C}, device_id_type=MESH)
    pl.semaphore_wait(barrier, R - 1 + C - 1)

    c_feat.wait()
    fcopies = []
    for o in range(1, Ro):
        cp = remote(xs.at[r], xs.at[r], fs.at[o], fr.at[r], ((yo + o) % Ro) * 2 + k, c)
        cp.start()
        fcopies.append(cp)
    cp = remote(xs.at[r], xs.at[r], fs.at[0], fr.at[r], inner, c)
    cp.start()
    fcopies.append(cp)

    tiles[S] = jnp.zeros((T, T), BF16)
    total = tcnt[0, 0]

    def set_pos(s, _):
        pos[s] = jnp.where(s < total, trow[0, 0, s] * R + tcol[0, 0, s], -1)
        return 0

    lax.fori_loop(0, S, set_pos, 0)

    def set_inv(p, _):
        slot = jnp.int32(S)
        for s in range(S):
            slot = jnp.where(pos[s] == p, jnp.int32(s), slot)
        inv[p] = slot
        return 0

    lax.fori_loop(0, C * R, set_inv, 0)

    for o in range(1, Ro):
        j = ((yo - o + Ro) % Ro) * 2 + k
        arrived(xs.at[j], fr.at[j])
        cp = remote(xs.at[j], xs.at[j], fs.at[Ro - 1 + o], fr.at[j], inner, c)
        cp.start()
        fcopies.append(cp)
    arrived(xs.at[inner], fr.at[inner])
    c_adj.wait()
    for o in range(1, Ro):
        j = ((yo - o + Ro) % Ro) * 2 + 1 - k
        arrived(xs.at[j], fr.at[j])

    tables = [sorted(range(Z), key=lambda d, zz=zz: (-abs(d - zz), d)) for zz in range(Z)]
    order = []
    for kk in range(Z):
        v = jnp.int32(tables[0][kk])
        for zz in range(1, Z):
            v = jnp.where(z == zz, jnp.int32(tables[zz][kk]), v)
        order.append(v)

    def pick(n):
        v = order[0]
        for kk in range(1, Z):
            v = jnp.where(n == kk, order[kk], v)
        return v

    def partial(i):
        total = dot(tiles[inv[i * R]], xs[0])
        for j in range(1, R):
            total += dot(tiles[inv[i * R + j]], xs[j])
        return total

    def px(n):
        return remote(xsend.at[n], xrecv.at[n], ps.at[n], pr.at[n], r, xpeer)

    def fwd_peer(n, _):
        xsend[n] = partial(pick(n) * 2 + 1 - x).astype(BF16)
        px(n).start()
        return 0

    lax.fori_loop(0, Z, fwd_peer, 0)

    def pz(n, d):
        right = d > z
        way = jnp.where(right, 0, 1)
        nxt = jnp.where(right, z + 1, z - 1)
        return remote(zsend.at[n], zrecv.at[way, d], zs.at[n], zr.at[way, d], r, nxt * 2 + x)

    def fwd_chain(n, _):
        d = pick(n)
        accf[...] = partial(d * 2 + x)
        arrived(xrecv.at[n], pr.at[n])
        accf[...] += xrecv[n].astype(F32)

        @pl.when((d >= z) & (z > 0))
        def _():
            arrived(zrecv.at[0, d], zr.at[0, d])
            accf[...] += zrecv[0, d].astype(F32)

        @pl.when((d <= z) & (z < Z - 1))
        def _():
            arrived(zrecv.at[1, d], zr.at[1, d])
            accf[...] += zrecv[1, d].astype(F32)

        @pl.when(d != z)
        def _():
            zsend[n] = accf[...].astype(BF16)
            pz(n, d).start()

        return 0

    lax.fori_loop(0, Z, fwd_chain, 0)

    c_w.wait()
    c_g.wait()
    agg = accf[...].astype(BF16)
    pre = dot(agg, wv[...])
    sig = jax.nn.sigmoid(pre)
    grad = (gv[...].astype(F32) * sig * (1.0 + pre * (1.0 - sig))).astype(BF16)
    mt[c] = lax.dot_general(
        wv[...], grad, (((1,), (1,)), ((), ())), preferred_element_type=F32).astype(BF16)

    def to_right(n, s):
        i = s * 2 + x
        return remote(mt.at[i], mt.at[i], ms.at[0, n], mr.at[i], r, (z + 1) * 2 + x)

    def to_left(n, s):
        i = s * 2 + x
        return remote(mt.at[i], mt.at[i], ms.at[1, n], mr.at[i], r, (z - 1) * 2 + x)

    def to_peer(n, s):
        i = s * 2 + x
        return remote(mt.at[i], mt.at[i], ms.at[2, n], mr.at[i], r, xpeer)

    def spread(n, s, act):
        @pl.when((s <= z) & (z < Z - 1))
        def _():
            act(to_right(n, s))

        @pl.when((s >= z) & (z > 0))
        def _():
            act(to_left(n, s))

        act(to_peer(n, s))

    spread(0, z, lambda cp: cp.start())

    actv[...] = (pre * sig).astype(BF16)
    c_act = pltpu.make_async_copy(actv, act_out, loc.at[4])
    c_act.start()

    aggt = jnp.transpose(agg.astype(F32)).astype(BF16)
    wterm[...] = dot(aggt, grad).astype(BF16)
    w1copies = []
    for o in range(1, C):
        to = (c + o) % C
        cp = remote(wterm.at[pl.ds(pl.multiple_of(to * H, H), H)], wr1.at[o], w1s.at[o],
                    w1r.at[o], r, to)
        cp.start()
        w1copies.append(cp)

    for j in range(R):
        bacc[j] = jnp.zeros((F, T), F32)

    def bwd_step(n):
        @pl.when((n > 0) & (n < Z))
        def _():
            s = pick(Z - 1 - n)
            i = s * 2 + x
            arrived(mt.at[i], mr.at[i])
            spread(n, s, lambda cp: cp.start())

        def half(h, _):
            m = n - h

            @pl.when((m >= 0) & (m < Z))
            def _():
                s = pick(Z - 1 - m)
                i = s * 2 + jnp.where(h == 0, x, 1 - x)

                @pl.when(h == 1)
                def _():
                    arrived(mt.at[i], mr.at[i])

                for j in range(R):
                    bacc[j] += dot(mt[i], tiles[inv[i * R + j]])

            return 0

        lax.fori_loop(0, 2, half, 0)

    def bwd_loop(n, _):
        bwd_step(n)

        @pl.when(n == Z - 1)
        def _():
            sel = wterm[pl.ds(pl.multiple_of(c * H, H), H), :].astype(F32)
            for o in range(1, C):
                arrived(wr1.at[o], w1r.at[o])
                sel += wr1[o].astype(F32)
            wr2[r] = sel.astype(BF16)
            for o in range(1, R):
                remote(wr2.at[r], wr2.at[r], w2s.at[o], w2r.at[r], (r + o) % R, c).start()

        return 0

    lax.fori_loop(0, Z + 1, bwd_loop, 0)

    def bx(o):
        to = (yo + o) % Ro
        return remote(bsend.at[o], brecv.at[o], bs.at[o], br.at[o], r - r % 2 + 1 - k, c)

    for o in list(range(1, Ro)) + [0]:
        to = (yo + o) % Ro
        bsend[o] = bacc[to * 2 + 1 - k].astype(BF16)
        bx(o).start()
    bcopies = []
    for o in range(1, Ro):
        to = (yo + o) % Ro
        arrived(brecv.at[o], br.at[o])
        osend[o] = (bacc[to * 2 + k] + brecv[o].astype(F32)).astype(BF16)
        cp = remote(osend.at[o], orecv.at[o], os_.at[o], or_.at[o], to * 2 + k, c)
        cp.start()
        bcopies.append(cp)

    for o in range(1, R):
        arrived(wr2.at[(r + o) % R], w2r.at[(r + o) % R])
    sel = wr2[0].astype(F32)
    for j in range(1, R):
        sel += wr2[j].astype(F32)
    wr3[pl.ds(pl.multiple_of(c * H, H), H), :] = (sel * scale).astype(BF16)
    mine = wr3.at[pl.ds(pl.multiple_of(c * H, H), H)]
    w3copies = []
    for o in range(1, C):
        cp = remote(mine, mine, w3s.at[o], w3r.at[c], r, (c + o) % C)
        cp.start()
        w3copies.append(cp)

    arrived(brecv.at[0], br.at[0])
    xg = bacc[r] + brecv[0].astype(F32)
    for o in range(1, Ro):
        arrived(orecv.at[o], or_.at[o])
        xg += orecv[o].astype(F32)
    xgv[...] = jnp.transpose(xg).astype(BF16)
    c_xg = pltpu.make_async_copy(xgv, xg_out, loc.at[5])
    c_xg.start()

    for o in range(1, C):
        src = (c + o) % C
        arrived(wr3.at[pl.ds(pl.multiple_of(src * H, H), H)], w3r.at[src])
    wgv[...] = wr3[...].astype(F32)
    c_wg = pltpu.make_async_copy(wgv, wg_out, loc.at[6])
    c_wg.start()

    for cp in fcopies:
        cp.wait_send()

    def sent(n, _):
        px(n).wait_send()
        d = pick(n)

        @pl.when(d != z)
        def _():
            pz(n, d).wait_send()

        spread(n, pick(Z - 1 - n), lambda cp: cp.wait_send())
        return 0

    lax.fori_loop(0, Z, sent, 0)
    for cp in w1copies + w3copies + bcopies:
        cp.wait_send()
    for o in range(1, R):
        remote(wr2.at[r], wr2.at[r], w2s.at[o], w2r.at[r], (r + o) % R, c).wait_send()
    for o in range(Ro):
        bx(o).wait_send()
    c_act.wait()
    c_xg.wait()
    c_wg.wait()


def local(features, adj_tiles, tile_rows, tile_cols, tile_count, weight, grad_out):
    R, C = lax.axis_size("row"), lax.axis_size("col")
    S, T = adj_tiles.shape[2], adj_tiles.shape[3]
    B, F = features.shape
    assert B == T and R % 2 == 0 and C % 2 == 0 and T % (16 * C) == 0
    Ro, Z = R // 2, C // 2
    H = T // C
    any_space = pl.BlockSpec(memory_space=pl.ANY)
    smem = pl.BlockSpec(memory_space=pltpu.SMEM)
    V = pltpu.VMEM
    dma = pltpu.SemaphoreType.DMA
    return pl.pallas_call(
        functools.partial(kernel, R, C, S, T, F, 1.0 / math.sqrt(B * R * C)),
        out_shape=(
            jax.ShapeDtypeStruct((B, F), BF16),
            jax.ShapeDtypeStruct((F, F), F32),
            jax.ShapeDtypeStruct((B, F), BF16),
        ),
        in_specs=[any_space, any_space, smem, smem, smem, any_space, any_space],
        out_specs=(any_space, any_space, any_space),
        scratch_shapes=[
            V((S + 1, T, T), BF16), V((R, T, F), BF16), V((F, F), BF16), V((T, F), BF16),
            pltpu.SMEM((S,), jnp.int32), pltpu.SMEM((C * R,), jnp.int32), V((T, F), F32),
            V((Z, T, F), BF16), V((Z, T, F), BF16), V((Z, T, F), BF16), V((2, Z, T, F), BF16),
            V((T, F), BF16), V((C, F, T), BF16), V((R, F, T), F32),
            V((Ro, F, T), BF16), V((Ro, F, T), BF16), V((Ro, F, T), BF16), V((Ro, F, T), BF16),
            V((T, F), BF16),
            V((F, F), BF16), V((C, H, F), BF16), V((R, H, F), BF16), V((F, F), BF16),
            V((F, F), F32),
            dma((7,)), dma((2 * Ro,)), dma((R,)), dma((Z,)), dma((Z,)), dma((Z,)), dma((2, Z)),
            dma((3, Z)), dma((C,)), dma((Ro,)), dma((Ro,)), dma((Ro,)), dma((Ro,)),
            dma((C,)), dma((C,)), dma((R,)), dma((R,)), dma((C,)), dma((C,)),
        ],
        compiler_params=pltpu.CompilerParams(
            collective_id=0, has_side_effects=True, vmem_limit_bytes=50 * 1024 * 1024,
        ),
        cost_estimate=pl.CostEstimate(
            flops=4 * C * R * T * T * F, bytes_accessed=2 * S * T * T, transcendentals=T * F),
    )(features, adj_tiles, tile_rows, tile_cols, tile_count, weight, grad_out)


def solution(mesh):
    return jax.shard_map(
        local,
        mesh=mesh,
        in_specs=(
            P(("col", "row"), None),
            P("row", "col", None, None, None),
            P("row", "col", None),
            P("row", "col", None),
            P("row", "col"),
            P(),
            P(("row", "col"), None),
        ),
        out_specs=(P(("row", "col"), None), P(), P(("col", "row"), None)),
        check_vma=False,
    )
```

```python
import functools
import math

import jax
import jax.numpy as jnp
from jax import lax
from jax.experimental import pallas as pl
from jax.experimental.pallas import tpu as pltpu
from jax.sharding import PartitionSpec as P

MESH = pl.DeviceIdType.MESH
BF16 = jnp.bfloat16
F32 = jnp.float32
Q = 2


def dot(a, b):
    return jnp.dot(a, b, preferred_element_type=F32)


def kernel(
    R, C, S, T, F, scale,
    feat, adj, trow, tcol, tcnt, wt, gout,
    act_out, wg_out, xg_out,
    tiles, xs, wv, gv, rows_s, cols_s, cnt_s, pos, inv, accf,
    xsend, xrecv, zsend, zrecv, actv, mt, bacc,
    bsend, brecv, osend, orecv, xgv,
    wterm, wr1, wr2, wr3, wgv,
    loc, fs, fr, ps, pr, zs, zr, ms, mr, bs, br, os_, or_,
    w1s, w1r, w2s, w2r, w3s, w3r,
):
    r = lax.axis_index("row")
    c = lax.axis_index("col")
    Ro, Z = R // 2, C // 2
    yo, k = r // 2, r % 2
    z, x = c // 2, c % 2
    inner = yo * 2 + 1 - k
    xpeer = z * 2 + 1 - x
    H = T // C

    def remote(src, dst, ss, rs, row, col):
        return pltpu.make_async_remote_copy(
            src_ref=src, dst_ref=dst, send_sem=ss, recv_sem=rs,
            device_id={"row": row, "col": col}, device_id_type=MESH,
        )

    def arrived(dst, rs):
        pltpu.make_async_copy(dst, dst, rs).wait()

    c_feat = pltpu.make_async_copy(feat, xs.at[r], loc.at[0])
    c_feat.start()
    c_adj = pltpu.make_async_copy(adj.at[0, 0], tiles.at[pl.ds(0, S)], loc.at[1])
    c_adj.start()
    c_w = pltpu.make_async_copy(wt, wv, loc.at[2])
    c_w.start()
    c_g = pltpu.make_async_copy(gout, gv, loc.at[3])
    c_g.start()

    c_ids = [
        pltpu.make_async_copy(src, dst, loc.at[7 + n])
        for n, (src, dst) in enumerate(((trow, rows_s), (tcol, cols_s), (tcnt, cnt_s)))
    ]
    for cp in c_ids:
        cp.start()

    barrier = pltpu.get_barrier_semaphore()
    for o in range(1, R):
        pl.semaphore_signal(
            barrier, inc=1, device_id={"row": (r + o) % R, "col": c}, device_id_type=MESH)
    for o in range(1, C):
        pl.semaphore_signal(
            barrier, inc=1, device_id={"row": r, "col": (c + o) % C}, device_id_type=MESH)
    pl.semaphore_wait(barrier, R - 1 + C - 1)

    c_feat.wait()
    fcopies = []
    for o in range(1, Ro):
        cp = remote(xs.at[r], xs.at[r], fs.at[o], fr.at[r], ((yo + o) % Ro) * 2 + k, c)
        cp.start()
        fcopies.append(cp)
    cp = remote(xs.at[r], xs.at[r], fs.at[0], fr.at[r], inner, c)
    cp.start()
    fcopies.append(cp)

    tiles[S] = jnp.zeros((T, T), BF16)
    for cp in c_ids:
        cp.wait()
    total = cnt_s[0, 0]

    def set_pos(s, _):
        pos[s] = jnp.where(s < total, rows_s[0, 0, s] * R + cols_s[0, 0, s], -1)
        return 0

    lax.fori_loop(0, S, set_pos, 0)

    def set_inv(p, _):
        slot = jnp.int32(S)
        for s in range(S):
            slot = jnp.where(pos[s] == p, jnp.int32(s), slot)
        inv[p] = slot
        return 0

    lax.fori_loop(0, C * R, set_inv, 0)

    for o in range(1, Ro):
        j = ((yo - o + Ro) % Ro) * 2 + k
        arrived(xs.at[j], fr.at[j])
        cp = remote(xs.at[j], xs.at[j], fs.at[Ro - 1 + o], fr.at[j], inner, c)
        cp.start()
        fcopies.append(cp)
    arrived(xs.at[inner], fr.at[inner])
    c_adj.wait()
    for o in range(1, Ro):
        j = ((yo - o + Ro) % Ro) * 2 + 1 - k
        arrived(xs.at[j], fr.at[j])

    tables = [sorted(range(Z), key=lambda d, zz=zz: (-abs(d - zz), d)) for zz in range(Z)]
    order = []
    for kk in range(Z):
        v = jnp.int32(tables[0][kk])
        for zz in range(1, Z):
            v = jnp.where(z == zz, jnp.int32(tables[zz][kk]), v)
        order.append(v)

    def pick(n):
        v = order[0]
        for kk in range(1, Z):
            v = jnp.where(n == kk, order[kk], v)
        return v

    def partial(i):
        total = dot(tiles[inv[i * R]], xs[0])
        for j in range(1, R):
            total += dot(tiles[inv[i * R + j]], xs[j])
        return total

    def px(n, q):
        return remote(xsend.at[n, q], xrecv.at[n, q], ps.at[n, q], pr.at[n, q], r, xpeer)

    def fwd_peer(n, _):
        xsend[n] = partial(pick(n) * 2 + 1 - x).astype(BF16).reshape(Q, T // Q, F)
        for q in range(Q):
            px(n, q).start()
        return 0

    lax.fori_loop(0, Z, fwd_peer, 0)

    def pz(n, d, q):
        right = d > z
        way = jnp.where(right, 0, 1)
        nxt = jnp.where(right, z + 1, z - 1)
        return remote(zsend.at[n, q], zrecv.at[way, d, q], zs.at[n, q], zr.at[way, d, q], r,
                      nxt * 2 + x)

    def fwd_chain(n, _):
        d = pick(n)
        accf[...] = partial(d * 2 + x).reshape(Q, T // Q, F)

        def piece(q, _):
            arrived(xrecv.at[n, q], pr.at[n, q])
            accf[q] += xrecv[n, q].astype(F32)

            @pl.when((d >= z) & (z > 0))
            def _():
                arrived(zrecv.at[0, d, q], zr.at[0, d, q])
                accf[q] += zrecv[0, d, q].astype(F32)

            @pl.when((d <= z) & (z < Z - 1))
            def _():
                arrived(zrecv.at[1, d, q], zr.at[1, d, q])
                accf[q] += zrecv[1, d, q].astype(F32)

            @pl.when(d != z)
            def _():
                zsend[n, q] = accf[q].astype(BF16)
                pz(n, d, q).start()

            return 0

        lax.fori_loop(0, Q, piece, 0)
        return 0

    lax.fori_loop(0, Z, fwd_chain, 0)

    c_w.wait()
    c_g.wait()
    agg = accf[...].reshape(T, F).astype(BF16)
    pre = dot(agg, wv[...])
    sig = jax.nn.sigmoid(pre)
    grad = (gv[...].astype(F32) * sig * (1.0 + pre * (1.0 - sig))).astype(BF16)
    mt[c] = lax.dot_general(
        wv[...], grad, (((1,), (1,)), ((), ())), preferred_element_type=F32
    ).astype(BF16).reshape(Q, F // Q, T)

    def to_z(n, s, q, way):
        i = s * 2 + x
        return remote(mt.at[i, q], mt.at[i, q], ms.at[way, n, q], mr.at[i, q], r,
                      (z + 1 - 2 * way) * 2 + x)

    def to_peer(n, s, q):
        i = s * 2 + x
        return remote(mt.at[i, q], mt.at[i, q], ms.at[2, n, q], mr.at[i, q], r, xpeer)

    def spread(n, s, q, act):
        @pl.when((s <= z) & (z < Z - 1))
        def _():
            act(to_z(n, s, q, 0))

        @pl.when((s >= z) & (z > 0))
        def _():
            act(to_z(n, s, q, 1))

        act(to_peer(n, s, q))

    for q in range(Q):
        spread(0, z, q, lambda cp: cp.start())

    actv[...] = (pre * sig).astype(BF16)
    c_act = pltpu.make_async_copy(actv, act_out, loc.at[4])
    c_act.start()

    aggt = jnp.transpose(agg.astype(F32)).astype(BF16)
    wterm[...] = dot(aggt, grad).astype(BF16)
    w1copies = []
    for o in range(1, C):
        to = (c + o) % C
        cp = remote(wterm.at[pl.ds(pl.multiple_of(to * H, H), H)], wr1.at[o], w1s.at[o],
                    w1r.at[o], r, to)
        cp.start()
        w1copies.append(cp)

    for j in range(R):
        bacc[j] = jnp.zeros((F, T), F32)

    def bwd_step(n):
        @pl.when((n > 0) & (n < Z))
        def _():
            s = pick(Z - 1 - n)
            i = s * 2 + x
            for q in range(Q):
                arrived(mt.at[i, q], mr.at[i, q])
                spread(n, s, q, lambda cp: cp.start())

        def half(h, _):
            m = n - h

            @pl.when((m >= 0) & (m < Z))
            def _():
                s = pick(Z - 1 - m)
                i = s * 2 + jnp.where(h == 0, x, 1 - x)

                @pl.when(h == 1)
                def _():
                    for q in range(Q):
                        arrived(mt.at[i, q], mr.at[i, q])

                for j in range(R):
                    bacc[j] += dot(mt[i].reshape(F, T), tiles[inv[i * R + j]])

            return 0

        lax.fori_loop(0, 2, half, 0)

    def bwd_loop(n, _):
        bwd_step(n)

        @pl.when(n == Z - 1)
        def _():
            sel = wterm[pl.ds(pl.multiple_of(c * H, H), H), :].astype(F32)
            for o in range(1, C):
                arrived(wr1.at[o], w1r.at[o])
                sel += wr1[o].astype(F32)
            wr2[r] = sel.astype(BF16)
            for o in range(1, R):
                remote(wr2.at[r], wr2.at[r], w2s.at[o], w2r.at[r], (r + o) % R, c).start()

        return 0

    lax.fori_loop(0, Z + 1, bwd_loop, 0)

    def bx(o):
        to = (yo + o) % Ro
        return remote(bsend.at[o], brecv.at[o], bs.at[o], br.at[o], r - r % 2 + 1 - k, c)

    for o in list(range(1, Ro)) + [0]:
        to = (yo + o) % Ro
        bsend[o] = bacc[to * 2 + 1 - k].astype(BF16)
        bx(o).start()
    bcopies = []
    for o in range(1, Ro):
        to = (yo + o) % Ro
        arrived(brecv.at[o], br.at[o])
        osend[o] = (bacc[to * 2 + k] + brecv[o].astype(F32)).astype(BF16)
        cp = remote(osend.at[o], orecv.at[o], os_.at[o], or_.at[o], to * 2 + k, c)
        cp.start()
        bcopies.append(cp)

    for o in range(1, R):
        arrived(wr2.at[(r + o) % R], w2r.at[(r + o) % R])
    sel = wr2[0].astype(F32)
    for j in range(1, R):
        sel += wr2[j].astype(F32)
    wr3[pl.ds(pl.multiple_of(c * H, H), H), :] = (sel * scale).astype(BF16)
    mine = wr3.at[pl.ds(pl.multiple_of(c * H, H), H)]
    w3copies = []
    for o in range(1, C):
        cp = remote(mine, mine, w3s.at[o], w3r.at[c], r, (c + o) % C)
        cp.start()
        w3copies.append(cp)

    arrived(brecv.at[0], br.at[0])
    xg = bacc[r] + brecv[0].astype(F32)
    for o in range(1, Ro):
        arrived(orecv.at[o], or_.at[o])
        xg += orecv[o].astype(F32)
    xgv[...] = jnp.transpose(xg).astype(BF16)
    c_xg = pltpu.make_async_copy(xgv, xg_out, loc.at[5])
    c_xg.start()

    for o in range(1, C):
        src = (c + o) % C
        arrived(wr3.at[pl.ds(pl.multiple_of(src * H, H), H)], w3r.at[src])
    wgv[...] = wr3[...].astype(F32)
    c_wg = pltpu.make_async_copy(wgv, wg_out, loc.at[6])
    c_wg.start()

    for cp in fcopies:
        cp.wait_send()

    def sent(n, _):
        d = pick(n)
        for q in range(Q):
            px(n, q).wait_send()

            @pl.when(d != z)
            def _():
                pz(n, d, q).wait_send()

            spread(n, pick(Z - 1 - n), q, lambda cp: cp.wait_send())

        return 0

    lax.fori_loop(0, Z, sent, 0)
    for cp in w1copies + w3copies + bcopies:
        cp.wait_send()
    for o in range(1, R):
        remote(wr2.at[r], wr2.at[r], w2s.at[o], w2r.at[r], (r + o) % R, c).wait_send()
    for o in range(Ro):
        bx(o).wait_send()
    c_act.wait()
    c_xg.wait()
    c_wg.wait()


def hand_out(*refs):
    sems = refs[-1]
    copies = [pltpu.make_async_copy(refs[n], refs[3 + n], sems.at[n]) for n in range(3)]
    for cp in copies:
        cp.start()
    for cp in copies:
        cp.wait()


def local(features, adj_tiles, tile_rows, tile_cols, tile_count, weight, grad_out):
    R, C = lax.axis_size("row"), lax.axis_size("col")
    S, T = adj_tiles.shape[2], adj_tiles.shape[3]
    B, F = features.shape
    assert B == T and R % 2 == 0 and C % 2 == 0 and T % (16 * C) == 0
    Ro, Z = R // 2, C // 2
    H = T // C
    hbm = pl.BlockSpec(memory_space=pltpu.HBM)
    any_space = pl.BlockSpec(memory_space=pl.ANY)
    V = pltpu.VMEM
    dma = pltpu.SemaphoreType.DMA
    outs = pl.pallas_call(
        functools.partial(kernel, R, C, S, T, F, 1.0 / math.sqrt(B * R * C)),
        out_shape=(
            jax.ShapeDtypeStruct((B, F), BF16),
            jax.ShapeDtypeStruct((F, F), F32),
            jax.ShapeDtypeStruct((B, F), BF16),
        ),
        in_specs=[hbm] * 7,
        out_specs=(any_space, any_space, any_space),
        scratch_shapes=[
            V((S + 1, T, T), BF16), V((R, T, F), BF16), V((F, F), BF16), V((T, F), BF16),
            pltpu.SMEM((1, 1, S), jnp.int32), pltpu.SMEM((1, 1, S), jnp.int32),
            pltpu.SMEM((1, 1), jnp.int32),
            pltpu.SMEM((S,), jnp.int32), pltpu.SMEM((C * R,), jnp.int32), V((Q, T // Q, F), F32),
            V((Z, Q, T // Q, F), BF16), V((Z, Q, T // Q, F), BF16), V((Z, Q, T // Q, F), BF16),
            V((2, Z, Q, T // Q, F), BF16),
            V((T, F), BF16), V((C, Q, F // Q, T), BF16), V((R, F, T), F32),
            V((Ro, F, T), BF16), V((Ro, F, T), BF16), V((Ro, F, T), BF16), V((Ro, F, T), BF16),
            V((T, F), BF16),
            V((F, F), BF16), V((C, H, F), BF16), V((R, H, F), BF16), V((F, F), BF16),
            V((F, F), F32),
            dma((10,)), dma((2 * Ro,)), dma((R,)), dma((Z, Q)), dma((Z, Q)), dma((Z, Q)),
            dma((2, Z, Q)), dma((3, Z, Q)), dma((C, Q)), dma((Ro,)), dma((Ro,)), dma((Ro,)), dma((Ro,)),
            dma((C,)), dma((C,)), dma((R,)), dma((R,)), dma((C,)), dma((C,)),
        ],
        compiler_params=pltpu.CompilerParams(
            collective_id=0, has_side_effects=True, vmem_limit_bytes=62 * 1024 * 1024,
        ),
        cost_estimate=pl.CostEstimate(
            flops=4 * C * R * T * T * F, bytes_accessed=2 * S * T * T, transcendentals=T * F),
    )(features, adj_tiles, tile_rows, tile_cols, tile_count, weight, grad_out)
    return pl.pallas_call(
        hand_out,
        out_shape=tuple(jax.ShapeDtypeStruct(o.shape, o.dtype) for o in outs),
        in_specs=[any_space] * 3,
        out_specs=(hbm,) * 3,
        scratch_shapes=[dma((3,))],
        compiler_params=pltpu.CompilerParams(vmem_limit_bytes=62 * 1024 * 1024),
    )(*outs)


def solution(mesh):
    return jax.shard_map(
        local,
        mesh=mesh,
        in_specs=(
            P(("col", "row"), None),
            P("row", "col", None, None, None),
            P("row", "col", None),
            P("row", "col", None),
            P("row", "col"),
            P(),
            P(("row", "col"), None),
        ),
        out_specs=(P(("row", "col"), None), P(), P(("col", "row"), None)),
        check_vma=False,
    )
```

```python
import functools
import math

import jax
import jax.numpy as jnp
from jax import lax
from jax.experimental import pallas as pl
from jax.experimental.pallas import tpu as pltpu
from jax.sharding import PartitionSpec as P

MESH = pl.DeviceIdType.MESH
BF16 = jnp.bfloat16
F32 = jnp.float32
Q = 2


def dot(a, b):
    return jnp.dot(a, b, preferred_element_type=F32)


def kernel(
    R, C, S, T, F, scale,
    feat, adj, trow, tcol, tcnt, wt, gout,
    act_out, wg_out, xg_out,
    tiles, xs, wv, gv, rows_s, cols_s, cnt_s, pos, inv, accf,
    xsend, xrecv, zsend, zrecv, actv, aggv, gradv, mt, bacc,
    bsend, brecv, osend, orecv, xgv,
    wterm, wr1, wr2, wr3, wgv,
    loc, fs, fr, ps, pr, zs, zr, ms, mr, bs, br, os_, or_,
    w1s, w1r, w2s, w2r, w3s, w3r,
):
    r = lax.axis_index("row")
    c = lax.axis_index("col")
    Ro, Z = R // 2, C // 2
    yo, k = r // 2, r % 2
    z, x = c // 2, c % 2
    inner = yo * 2 + 1 - k
    xpeer = z * 2 + 1 - x
    H = T // C

    def remote(src, dst, ss, rs, row, col):
        return pltpu.make_async_remote_copy(
            src_ref=src, dst_ref=dst, send_sem=ss, recv_sem=rs,
            device_id={"row": row, "col": col}, device_id_type=MESH,
        )

    def arrived(dst, rs):
        pltpu.make_async_copy(dst, dst, rs).wait()

    c_feat = pltpu.make_async_copy(feat, xs.at[r], loc.at[0])
    c_feat.start()
    c_adj = pltpu.make_async_copy(adj.at[0, 0], tiles.at[pl.ds(0, S)], loc.at[1])
    c_adj.start()
    c_w = pltpu.make_async_copy(wt, wv, loc.at[2])
    c_w.start()
    c_g = pltpu.make_async_copy(gout, gv, loc.at[3])
    c_g.start()

    c_ids = [
        pltpu.make_async_copy(src, dst, loc.at[7 + n])
        for n, (src, dst) in enumerate(((trow, rows_s), (tcol, cols_s), (tcnt, cnt_s)))
    ]
    for cp in c_ids:
        cp.start()

    barrier = pltpu.get_barrier_semaphore()
    for o in range(1, R):
        pl.semaphore_signal(
            barrier, inc=1, device_id={"row": (r + o) % R, "col": c}, device_id_type=MESH)
    for o in range(1, C):
        pl.semaphore_signal(
            barrier, inc=1, device_id={"row": r, "col": (c + o) % C}, device_id_type=MESH)
    pl.semaphore_wait(barrier, R - 1 + C - 1)

    c_feat.wait()
    fcopies = []
    for o in range(1, Ro):
        cp = remote(xs.at[r], xs.at[r], fs.at[o], fr.at[r], ((yo + o) % Ro) * 2 + k, c)
        cp.start()
        fcopies.append(cp)
    cp = remote(xs.at[r], xs.at[r], fs.at[0], fr.at[r], inner, c)
    cp.start()
    fcopies.append(cp)

    tiles[S] = jnp.zeros((T, T), BF16)
    for cp in c_ids:
        cp.wait()
    total = cnt_s[0, 0]

    def set_pos(s, _):
        pos[s] = jnp.where(s < total, rows_s[0, 0, s] * R + cols_s[0, 0, s], -1)
        return 0

    lax.fori_loop(0, S, set_pos, 0)

    def set_inv(p, _):
        slot = jnp.int32(S)
        for s in range(S):
            slot = jnp.where(pos[s] == p, jnp.int32(s), slot)
        inv[p] = slot
        return 0

    lax.fori_loop(0, C * R, set_inv, 0)

    for o in range(1, Ro):
        j = ((yo - o + Ro) % Ro) * 2 + k
        arrived(xs.at[j], fr.at[j])
        cp = remote(xs.at[j], xs.at[j], fs.at[Ro - 1 + o], fr.at[j], inner, c)
        cp.start()
        fcopies.append(cp)
    arrived(xs.at[inner], fr.at[inner])
    c_adj.wait()
    for o in range(1, Ro):
        j = ((yo - o + Ro) % Ro) * 2 + 1 - k
        arrived(xs.at[j], fr.at[j])

    tables = [sorted(range(Z), key=lambda d, zz=zz: (-abs(d - zz), d)) for zz in range(Z)]
    order = []
    for kk in range(Z):
        v = jnp.int32(tables[0][kk])
        for zz in range(1, Z):
            v = jnp.where(z == zz, jnp.int32(tables[zz][kk]), v)
        order.append(v)

    def pick(n):
        v = order[0]
        for kk in range(1, Z):
            v = jnp.where(n == kk, order[kk], v)
        return v

    def partial(i):
        total = dot(tiles[inv[i * R]], xs[0])
        for j in range(1, R):
            total += dot(tiles[inv[i * R + j]], xs[j])
        return total

    def px(n, q):
        return remote(xsend.at[n, q], xrecv.at[n, q], ps.at[n, q], pr.at[n, q], r, xpeer)

    def fwd_peer(n, _):
        xsend[n] = partial(pick(n) * 2 + 1 - x).astype(BF16).reshape(Q, T // Q, F)
        px(n, 0).start()
        return 0

    lax.fori_loop(0, Z, fwd_peer, 0)

    def fwd_later(m, _):
        px(m % Z, m // Z).start()
        return 0

    lax.fori_loop(Z, Q * Z, fwd_later, 0)

    def pz(n, d, q):
        right = d > z
        way = jnp.where(right, 0, 1)
        nxt = jnp.where(right, z + 1, z - 1)
        return remote(zsend.at[n, q], zrecv.at[way, d, q], zs.at[n, q], zr.at[way, d, q], r,
                      nxt * 2 + x)

    def piece(n, q):
        d = pick(n)
        arrived(xrecv.at[n, q], pr.at[n, q])
        accf[n, q] += xrecv[n, q].astype(F32)

        @pl.when((d >= z) & (z > 0))
        def _():
            arrived(zrecv.at[0, d, q], zr.at[0, d, q])
            accf[n, q] += zrecv[0, d, q].astype(F32)

        @pl.when((d <= z) & (z < Z - 1))
        def _():
            arrived(zrecv.at[1, d, q], zr.at[1, d, q])
            accf[n, q] += zrecv[1, d, q].astype(F32)

        @pl.when(d != z)
        def _():
            zsend[n, q] = accf[n, q].astype(BF16)
            pz(n, d, q).start()

    def fwd_chain(m, _):
        q, n = m // Z, m % Z

        @pl.when(q == 0)
        def _():
            accf[n] = partial(pick(n) * 2 + x).reshape(Q, T // Q, F)

        @pl.when(n < Z - 1)
        def _():
            piece(n, q)

        return 0

    lax.fori_loop(0, Q * Z, fwd_chain, 0)

    def to_z(n, s, q, way):
        i = s * 2 + x
        return remote(mt.at[i, q], mt.at[i, q], ms.at[way, n, q], mr.at[i, q], r,
                      (z + 1 - 2 * way) * 2 + x)

    def to_peer(n, s, q):
        i = s * 2 + x
        return remote(mt.at[i, q], mt.at[i, q], ms.at[2, n, q], mr.at[i, q], r, xpeer)

    def spread(n, s, q, act):
        @pl.when((s <= z) & (z < Z - 1))
        def _():
            act(to_z(n, s, q, 0))

        @pl.when((s >= z) & (z > 0))
        def _():
            act(to_z(n, s, q, 1))

        act(to_peer(n, s, q))

    c_w.wait()
    c_g.wait()

    def dense(q, _):
        piece(Z - 1, q)
        rows = pl.ds(pl.multiple_of(q * (T // Q), T // Q), T // Q)
        agg = accf[Z - 1, q].astype(BF16)
        pre = dot(agg, wv[...])
        sig = jax.nn.sigmoid(pre)
        grad = (gv[rows, :].astype(F32) * sig * (1.0 + pre * (1.0 - sig))).astype(BF16)
        mt[c, q] = lax.dot_general(
            wv[...], grad, (((1,), (1,)), ((), ())), preferred_element_type=F32).astype(BF16)
        spread(0, z, q, lambda cp: cp.start())
        aggv[rows, :] = agg
        gradv[rows, :] = grad
        actv[rows, :] = (pre * sig).astype(BF16)
        return 0

    lax.fori_loop(0, Q, dense, 0)
    c_act = pltpu.make_async_copy(actv, act_out, loc.at[4])
    c_act.start()

    aggt = jnp.transpose(aggv[...].astype(F32)).astype(BF16)
    wterm[...] = dot(aggt, gradv[...]).astype(BF16)
    w1copies = []
    for o in range(1, C):
        to = (c + o) % C
        cp = remote(wterm.at[pl.ds(pl.multiple_of(to * H, H), H)], wr1.at[o], w1s.at[o],
                    w1r.at[o], r, to)
        cp.start()
        w1copies.append(cp)

    for j in range(R):
        bacc[j] = jnp.zeros((F, T), F32)

    def bwd_step(m):
        @pl.when((m % Z > 0) & (m < Q * Z))
        def _():
            q, n = m // Z, m % Z
            s = pick(Z - 1 - n)
            i = s * 2 + x
            arrived(mt.at[i, q], mr.at[i, q])
            spread(n, s, q, lambda cp: cp.start())

        def half(h, _):
            @pl.when((m - h >= 0) & (m - h < Q * Z))
            def _():
                q, n = (m - h) // Z, (m - h) % Z
                s = pick(Z - 1 - n)
                i = s * 2 + jnp.where(h == 0, x, 1 - x)

                @pl.when(h == 1)
                def _():
                    arrived(mt.at[i, q], mr.at[i, q])

                rows = pl.ds(pl.multiple_of(q * (T // Q), T // Q), T // Q)
                for j in range(R):
                    bacc[j] += dot(mt[i, q], tiles[inv[i * R + j], rows, :])

            return 0

        lax.fori_loop(0, 2, half, 0)

    def bwd_loop(n, _):
        bwd_step(n)

        @pl.when(n == Q * Z - 1)
        def _():
            sel = wterm[pl.ds(pl.multiple_of(c * H, H), H), :].astype(F32)
            for o in range(1, C):
                arrived(wr1.at[o], w1r.at[o])
                sel += wr1[o].astype(F32)
            wr2[r] = sel.astype(BF16)
            for o in range(1, R):
                remote(wr2.at[r], wr2.at[r], w2s.at[o], w2r.at[r], (r + o) % R, c).start()

        return 0

    lax.fori_loop(0, Q * Z + 1, bwd_loop, 0)

    def bx(o):
        to = (yo + o) % Ro
        return remote(bsend.at[o], brecv.at[o], bs.at[o], br.at[o], r - r % 2 + 1 - k, c)

    for o in list(range(1, Ro)) + [0]:
        to = (yo + o) % Ro
        bsend[o] = bacc[to * 2 + 1 - k].astype(BF16)
        bx(o).start()
    bcopies = []
    for o in range(1, Ro):
        to = (yo + o) % Ro
        arrived(brecv.at[o], br.at[o])
        osend[o] = (bacc[to * 2 + k] + brecv[o].astype(F32)).astype(BF16)
        cp = remote(osend.at[o], orecv.at[o], os_.at[o], or_.at[o], to * 2 + k, c)
        cp.start()
        bcopies.append(cp)

    for o in range(1, R):
        arrived(wr2.at[(r + o) % R], w2r.at[(r + o) % R])
    sel = wr2[0].astype(F32)
    for j in range(1, R):
        sel += wr2[j].astype(F32)
    wr3[pl.ds(pl.multiple_of(c * H, H), H), :] = (sel * scale).astype(BF16)
    mine = wr3.at[pl.ds(pl.multiple_of(c * H, H), H)]
    w3copies = []
    for o in range(1, C):
        cp = remote(mine, mine, w3s.at[o], w3r.at[c], r, (c + o) % C)
        cp.start()
        w3copies.append(cp)

    arrived(brecv.at[0], br.at[0])
    xg = bacc[r] + brecv[0].astype(F32)
    for o in range(1, Ro):
        arrived(orecv.at[o], or_.at[o])
        xg += orecv[o].astype(F32)
    xgv[...] = jnp.transpose(xg).astype(BF16)
    c_xg = pltpu.make_async_copy(xgv, xg_out, loc.at[5])
    c_xg.start()

    for o in range(1, C):
        src = (c + o) % C
        arrived(wr3.at[pl.ds(pl.multiple_of(src * H, H), H)], w3r.at[src])
    wgv[...] = wr3[...].astype(F32)
    c_wg = pltpu.make_async_copy(wgv, wg_out, loc.at[6])
    c_wg.start()

    for cp in fcopies:
        cp.wait_send()

    def sent(n, _):
        d = pick(n)
        for q in range(Q):
            px(n, q).wait_send()

            @pl.when(d != z)
            def _():
                pz(n, d, q).wait_send()

            spread(n, pick(Z - 1 - n), q, lambda cp: cp.wait_send())

        return 0

    lax.fori_loop(0, Z, sent, 0)
    for cp in w1copies + w3copies + bcopies:
        cp.wait_send()
    for o in range(1, R):
        remote(wr2.at[r], wr2.at[r], w2s.at[o], w2r.at[r], (r + o) % R, c).wait_send()
    for o in range(Ro):
        bx(o).wait_send()
    c_act.wait()
    c_xg.wait()
    c_wg.wait()


def hand_out(*refs):
    held, sems = refs[6:9], refs[9]
    come = [pltpu.make_async_copy(refs[n], held[n], sems.at[n]) for n in range(3)]
    go = [pltpu.make_async_copy(held[n], refs[3 + n], sems.at[3 + n]) for n in range(3)]
    for cp in come:
        cp.start()
    for n in range(3):
        come[n].wait()
        go[n].start()
    for cp in go:
        cp.wait()


def local(features, adj_tiles, tile_rows, tile_cols, tile_count, weight, grad_out):
    R, C = lax.axis_size("row"), lax.axis_size("col")
    S, T = adj_tiles.shape[2], adj_tiles.shape[3]
    B, F = features.shape
    assert B == T and R % 2 == 0 and C % 2 == 0 and T % (16 * C) == 0
    Ro, Z = R // 2, C // 2
    H = T // C
    hbm = pl.BlockSpec(memory_space=pltpu.HBM)
    any_space = pl.BlockSpec(memory_space=pl.ANY)
    V = pltpu.VMEM
    dma = pltpu.SemaphoreType.DMA
    outs = pl.pallas_call(
        functools.partial(kernel, R, C, S, T, F, 1.0 / math.sqrt(B * R * C)),
        out_shape=(
            jax.ShapeDtypeStruct((B, F), BF16),
            jax.ShapeDtypeStruct((F, F), F32),
            jax.ShapeDtypeStruct((B, F), BF16),
        ),
        in_specs=[hbm] * 7,
        out_specs=(any_space, any_space, any_space),
        scratch_shapes=[
            V((S + 1, T, T), BF16), V((R, T, F), BF16), V((F, F), BF16), V((T, F), BF16),
            pltpu.SMEM((1, 1, S), jnp.int32), pltpu.SMEM((1, 1, S), jnp.int32),
            pltpu.SMEM((1, 1), jnp.int32),
            pltpu.SMEM((S,), jnp.int32), pltpu.SMEM((C * R,), jnp.int32), V((Z, Q, T // Q, F), F32),
            V((Z, Q, T // Q, F), BF16), V((Z, Q, T // Q, F), BF16), V((Z, Q, T // Q, F), BF16),
            V((2, Z, Q, T // Q, F), BF16),
            V((T, F), BF16), V((T, F), BF16), V((T, F), BF16), V((C, Q, F, T // Q), BF16), V((R, F, T), F32),
            V((Ro, F, T), BF16), V((Ro, F, T), BF16), V((Ro, F, T), BF16), V((Ro, F, T), BF16),
            V((T, F), BF16),
            V((F, F), BF16), V((C, H, F), BF16), V((R, H, F), BF16), V((F, F), BF16),
            V((F, F), F32),
            dma((10,)), dma((2 * Ro,)), dma((R,)), dma((Z, Q)), dma((Z, Q)), dma((Z, Q)),
            dma((2, Z, Q)), dma((3, Z, Q)), dma((C, Q)), dma((Ro,)), dma((Ro,)), dma((Ro,)), dma((Ro,)),
            dma((C,)), dma((C,)), dma((R,)), dma((R,)), dma((C,)), dma((C,)),
        ],
        compiler_params=pltpu.CompilerParams(
            collective_id=0, has_side_effects=True, vmem_limit_bytes=62 * 1024 * 1024,
        ),
        cost_estimate=pl.CostEstimate(
            flops=4 * C * R * T * T * F, bytes_accessed=2 * S * T * T, transcendentals=T * F),
    )(features, adj_tiles, tile_rows, tile_cols, tile_count, weight, grad_out)
    return pl.pallas_call(
        hand_out,
        out_shape=tuple(jax.ShapeDtypeStruct(o.shape, o.dtype) for o in outs),
        in_specs=[any_space] * 3,
        out_specs=(hbm,) * 3,
        scratch_shapes=[V(o.shape, o.dtype) for o in outs] + [dma((6,))],
        compiler_params=pltpu.CompilerParams(vmem_limit_bytes=62 * 1024 * 1024),
    )(*outs)


def solution(mesh):
    return jax.shard_map(
        local,
        mesh=mesh,
        in_specs=(
            P(("col", "row"), None),
            P("row", "col", None, None, None),
            P("row", "col", None),
            P("row", "col", None),
            P("row", "col"),
            P(),
            P(("row", "col"), None),
        ),
        out_specs=(P(("row", "col"), None), P(), P(("col", "row"), None)),
        check_vma=False,
    )
```

```python
import functools
import math

import jax
import jax.numpy as jnp
from jax import lax
from jax.experimental import pallas as pl
from jax.experimental.pallas import tpu as pltpu
from jax.sharding import PartitionSpec as P

MESH = pl.DeviceIdType.MESH
BF16 = jnp.bfloat16
F32 = jnp.float32
Q = 2


def dot(a, b):
    return jnp.dot(a, b, preferred_element_type=F32)


def kernel(
    R, C, S, T, F, scale,
    feat, adj, trow, tcol, tcnt, wt, gout,
    act_out, wg_out, xg_out,
    tiles, xs, wv, gv, rows_s, cols_s, cnt_s, pos, inv, accf,
    xsend, xrecv, zsend, zrecv, actv, aggv, gradv, mt, bacc,
    bsend, brecv, osend, orecv, xgv,
    wterm, wr1, wr2, wr3, wgv,
    loc, fs, fr, ps, pr, zs, zr, ms, mr, bs, br, os_, or_,
    w1s, w1r, w2s, w2r, w3s, w3r,
):
    r = lax.axis_index("row")
    c = lax.axis_index("col")
    Ro, Z = R // 2, C // 2
    yo, k = r // 2, r % 2
    z, x = c // 2, c % 2
    inner = yo * 2 + 1 - k
    xpeer = z * 2 + 1 - x
    H = T // C

    def remote(src, dst, ss, rs, row, col):
        return pltpu.make_async_remote_copy(
            src_ref=src, dst_ref=dst, send_sem=ss, recv_sem=rs,
            device_id={"row": row, "col": col}, device_id_type=MESH,
        )

    def arrived(dst, rs):
        pltpu.make_async_copy(dst, dst, rs).wait()

    c_feat = pltpu.make_async_copy(feat, xs.at[r], loc.at[0])
    c_feat.start()
    c_adj = pltpu.make_async_copy(adj.at[0, 0], tiles.at[pl.ds(0, S)], loc.at[1])
    c_adj.start()
    c_w = pltpu.make_async_copy(wt, wv, loc.at[2])
    c_w.start()
    c_g = pltpu.make_async_copy(gout, gv, loc.at[3])
    c_g.start()

    c_ids = [
        pltpu.make_async_copy(src, dst, loc.at[7 + n])
        for n, (src, dst) in enumerate(((trow, rows_s), (tcol, cols_s), (tcnt, cnt_s)))
    ]
    for cp in c_ids:
        cp.start()

    barrier = pltpu.get_barrier_semaphore()
    for o in range(1, R):
        pl.semaphore_signal(
            barrier, inc=1, device_id={"row": (r + o) % R, "col": c}, device_id_type=MESH)
    for o in range(1, C):
        pl.semaphore_signal(
            barrier, inc=1, device_id={"row": r, "col": (c + o) % C}, device_id_type=MESH)
    pl.semaphore_wait(barrier, R - 1 + C - 1)

    c_feat.wait()
    fcopies = []
    for o in range(1, Ro):
        cp = remote(xs.at[r], xs.at[r], fs.at[o], fr.at[r], ((yo + o) % Ro) * 2 + k, c)
        cp.start()
        fcopies.append(cp)
    cp = remote(xs.at[r], xs.at[r], fs.at[0], fr.at[r], inner, c)
    cp.start()
    fcopies.append(cp)

    tiles[S] = jnp.zeros((T, T), BF16)
    for cp in c_ids:
        cp.wait()
    total = cnt_s[0, 0]

    def set_pos(s, _):
        pos[s] = jnp.where(s < total, rows_s[0, 0, s] * R + cols_s[0, 0, s], -1)
        return 0

    lax.fori_loop(0, S, set_pos, 0)

    def set_inv(p, _):
        slot = jnp.int32(S)
        for s in range(S):
            slot = jnp.where(pos[s] == p, jnp.int32(s), slot)
        inv[p] = slot
        return 0

    lax.fori_loop(0, C * R, set_inv, 0)

    for o in range(1, Ro):
        j = ((yo - o + Ro) % Ro) * 2 + k
        arrived(xs.at[j], fr.at[j])
        cp = remote(xs.at[j], xs.at[j], fs.at[Ro - 1 + o], fr.at[j], inner, c)
        cp.start()
        fcopies.append(cp)
    arrived(xs.at[inner], fr.at[inner])
    c_adj.wait()
    for o in range(1, Ro):
        j = ((yo - o + Ro) % Ro) * 2 + 1 - k
        arrived(xs.at[j], fr.at[j])

    tables = [sorted(range(Z), key=lambda d, zz=zz: (-abs(d - zz), d)) for zz in range(Z)]
    order = []
    for kk in range(Z):
        v = jnp.int32(tables[0][kk])
        for zz in range(1, Z):
            v = jnp.where(z == zz, jnp.int32(tables[zz][kk]), v)
        order.append(v)

    def pick(n):
        v = order[0]
        for kk in range(1, Z):
            v = jnp.where(n == kk, order[kk], v)
        return v

    def partial(i):
        row = jnp.concatenate([tiles[inv[i * R + j]] for j in range(R)], axis=1)
        return dot(row, xs[...].reshape(R * T, F))

    def px(n, q):
        return remote(xsend.at[n, q], xrecv.at[n, q], ps.at[n, q], pr.at[n, q], r, xpeer)

    def fwd_peer(n, _):
        xsend[n] = partial(pick(n) * 2 + 1 - x).astype(BF16).reshape(Q, T // Q, F)
        px(n, 0).start()
        return 0

    lax.fori_loop(0, Z, fwd_peer, 0)

    def fwd_later(m, _):
        px(m % Z, m // Z).start()
        return 0

    lax.fori_loop(Z, Q * Z, fwd_later, 0)

    def pz(n, d, q):
        right = d > z
        way = jnp.where(right, 0, 1)
        nxt = jnp.where(right, z + 1, z - 1)
        return remote(zsend.at[n, q], zrecv.at[way, d, q], zs.at[n, q], zr.at[way, d, q], r,
                      nxt * 2 + x)

    def piece(n, q):
        d = pick(n)
        arrived(xrecv.at[n, q], pr.at[n, q])
        accf[n, q] += xrecv[n, q].astype(F32)

        @pl.when((d >= z) & (z > 0))
        def _():
            arrived(zrecv.at[0, d, q], zr.at[0, d, q])
            accf[n, q] += zrecv[0, d, q].astype(F32)

        @pl.when((d <= z) & (z < Z - 1))
        def _():
            arrived(zrecv.at[1, d, q], zr.at[1, d, q])
            accf[n, q] += zrecv[1, d, q].astype(F32)

        @pl.when(d != z)
        def _():
            zsend[n, q] = accf[n, q].astype(BF16)
            pz(n, d, q).start()

    def fwd_chain(m, _):
        q, n = m // Z, m % Z

        @pl.when(q == 0)
        def _():
            accf[n] = partial(pick(n) * 2 + x).reshape(Q, T // Q, F)

        @pl.when(n < Z - 1)
        def _():
            piece(n, q)

        return 0

    lax.fori_loop(0, Q * Z, fwd_chain, 0)

    def to_z(n, s, q, way):
        i = s * 2 + x
        return remote(mt.at[i, q], mt.at[i, q], ms.at[way, n, q], mr.at[i, q], r,
                      (z + 1 - 2 * way) * 2 + x)

    def to_peer(n, s, q):
        i = s * 2 + x
        return remote(mt.at[i, q], mt.at[i, q], ms.at[2, n, q], mr.at[i, q], r, xpeer)

    def spread(n, s, q, act):
        @pl.when((s <= z) & (z < Z - 1))
        def _():
            act(to_z(n, s, q, 0))

        @pl.when((s >= z) & (z > 0))
        def _():
            act(to_z(n, s, q, 1))

        act(to_peer(n, s, q))

    c_w.wait()
    c_g.wait()

    def dense(q, _):
        piece(Z - 1, q)
        rows = pl.ds(pl.multiple_of(q * (T // Q), T // Q), T // Q)
        agg = accf[Z - 1, q].astype(BF16)
        pre = dot(agg, wv[...])
        sig = jax.nn.sigmoid(pre)
        grad = (gv[rows, :].astype(F32) * sig * (1.0 + pre * (1.0 - sig))).astype(BF16)
        mt[c, q] = lax.dot_general(
            wv[...], grad, (((1,), (1,)), ((), ())), preferred_element_type=F32).astype(BF16)
        spread(0, z, q, lambda cp: cp.start())
        aggv[rows, :] = agg
        gradv[rows, :] = grad
        actv[rows, :] = (pre * sig).astype(BF16)
        return 0

    lax.fori_loop(0, Q, dense, 0)
    c_act = pltpu.make_async_copy(actv, act_out, loc.at[4])
    c_act.start()

    def to_row(o):
        to = (c + o) % C
        return remote(wterm.at[pl.ds(pl.multiple_of(to * H, H), H)], wr1.at[o], w1s.at[o],
                      w1r.at[o], r, to)

    def add_blocks(blocks, first):
        left = jnp.concatenate([mt[i, q] for i, q in blocks], axis=1)
        for j in range(R):
            right = jnp.concatenate(
                [
                    tiles[inv[i * R + j], pl.ds(pl.multiple_of(q * (T // Q), T // Q), T // Q), :]
                    for i, q in blocks
                ],
                axis=0,
            )
            if first:
                bacc[j] = dot(left, right)
            else:
                bacc[j] += dot(left, right)

    def block_of(m, side):
        return pick(Z - 1 - m % Z) * 2 + side, m // Z

    add_blocks([(c, 0)], True)

    def bwd_step(m, _):
        zi, zq = block_of(m, x)

        @pl.when(m % Z > 0)
        def _():
            arrived(mt.at[zi, zq], mr.at[zi, zq])
            spread(m % Z, zi // 2, zq, lambda cp: cp.start())

        xi, xq = block_of(m - 1, 1 - x)
        arrived(mt.at[xi, xq], mr.at[xi, xq])
        add_blocks([(zi, zq), (xi, xq)], False)

        @pl.when(m == 1)
        def _():
            aggt = jnp.transpose(aggv[...].astype(F32)).astype(BF16)
            wterm[...] = dot(aggt, gradv[...]).astype(BF16)
            for o in range(1, C):
                to_row(o).start()

        @pl.when(m == Q * Z - 1)
        def _():
            sel = wterm[pl.ds(pl.multiple_of(c * H, H), H), :].astype(F32)
            for o in range(1, C):
                arrived(wr1.at[o], w1r.at[o])
                sel += wr1[o].astype(F32)
            wr2[r] = sel.astype(BF16)
            for o in range(1, R):
                remote(wr2.at[r], wr2.at[r], w2s.at[o], w2r.at[r], (r + o) % R, c).start()

        return 0

    lax.fori_loop(1, Q * Z, bwd_step, 0)
    xi, xq = block_of(Q * Z - 1, 1 - x)
    arrived(mt.at[xi, xq], mr.at[xi, xq])
    add_blocks([(xi, xq)], False)

    def bx(o):
        to = (yo + o) % Ro
        return remote(bsend.at[o], brecv.at[o], bs.at[o], br.at[o], r - r % 2 + 1 - k, c)

    for o in list(range(1, Ro)) + [0]:
        to = (yo + o) % Ro
        bsend[o] = bacc[to * 2 + 1 - k].astype(BF16)
        bx(o).start()
    bcopies = []
    for o in range(1, Ro):
        to = (yo + o) % Ro
        arrived(brecv.at[o], br.at[o])
        osend[o] = (bacc[to * 2 + k] + brecv[o].astype(F32)).astype(BF16)
        cp = remote(osend.at[o], orecv.at[o], os_.at[o], or_.at[o], to * 2 + k, c)
        cp.start()
        bcopies.append(cp)

    for o in range(1, R):
        arrived(wr2.at[(r + o) % R], w2r.at[(r + o) % R])
    sel = wr2[0].astype(F32)
    for j in range(1, R):
        sel += wr2[j].astype(F32)
    wr3[pl.ds(pl.multiple_of(c * H, H), H), :] = (sel * scale).astype(BF16)
    mine = wr3.at[pl.ds(pl.multiple_of(c * H, H), H)]
    w3copies = []
    for o in range(1, C):
        cp = remote(mine, mine, w3s.at[o], w3r.at[c], r, (c + o) % C)
        cp.start()
        w3copies.append(cp)

    arrived(brecv.at[0], br.at[0])
    xg = bacc[r] + brecv[0].astype(F32)
    for o in range(1, Ro):
        arrived(orecv.at[o], or_.at[o])
        xg += orecv[o].astype(F32)
    xgv[...] = jnp.transpose(xg).astype(BF16)
    c_xg = pltpu.make_async_copy(xgv, xg_out, loc.at[5])
    c_xg.start()

    for o in range(1, C):
        src = (c + o) % C
        arrived(wr3.at[pl.ds(pl.multiple_of(src * H, H), H)], w3r.at[src])
    wgv[...] = wr3[...].astype(F32)
    c_wg = pltpu.make_async_copy(wgv, wg_out, loc.at[6])
    c_wg.start()

    for cp in fcopies:
        cp.wait_send()

    def sent(n, _):
        d = pick(n)
        for q in range(Q):
            px(n, q).wait_send()

            @pl.when(d != z)
            def _():
                pz(n, d, q).wait_send()

            spread(n, pick(Z - 1 - n), q, lambda cp: cp.wait_send())

        return 0

    lax.fori_loop(0, Z, sent, 0)
    for o in range(1, C):
        to_row(o).wait_send()
    for cp in w3copies + bcopies:
        cp.wait_send()
    for o in range(1, R):
        remote(wr2.at[r], wr2.at[r], w2s.at[o], w2r.at[r], (r + o) % R, c).wait_send()
    for o in range(Ro):
        bx(o).wait_send()
    c_act.wait()
    c_xg.wait()
    c_wg.wait()


def hand_out(*refs):
    held, sems = refs[6:9], refs[9]
    come = [pltpu.make_async_copy(refs[n], held[n], sems.at[n]) for n in range(3)]
    go = [pltpu.make_async_copy(held[n], refs[3 + n], sems.at[3 + n]) for n in range(3)]
    for cp in come:
        cp.start()
    for n in range(3):
        come[n].wait()
        go[n].start()
    for cp in go:
        cp.wait()


def local(features, adj_tiles, tile_rows, tile_cols, tile_count, weight, grad_out):
    R, C = lax.axis_size("row"), lax.axis_size("col")
    S, T = adj_tiles.shape[2], adj_tiles.shape[3]
    B, F = features.shape
    assert B == T and R % 2 == 0 and C % 2 == 0 and T % (16 * C) == 0
    Ro, Z = R // 2, C // 2
    H = T // C
    hbm = pl.BlockSpec(memory_space=pltpu.HBM)
    any_space = pl.BlockSpec(memory_space=pl.ANY)
    V = pltpu.VMEM
    dma = pltpu.SemaphoreType.DMA
    outs = pl.pallas_call(
        functools.partial(kernel, R, C, S, T, F, 1.0 / math.sqrt(B * R * C)),
        out_shape=(
            jax.ShapeDtypeStruct((B, F), BF16),
            jax.ShapeDtypeStruct((F, F), F32),
            jax.ShapeDtypeStruct((B, F), BF16),
        ),
        in_specs=[hbm] * 7,
        out_specs=(any_space, any_space, any_space),
        scratch_shapes=[
            V((S + 1, T, T), BF16), V((R, T, F), BF16), V((F, F), BF16), V((T, F), BF16),
            pltpu.SMEM((1, 1, S), jnp.int32), pltpu.SMEM((1, 1, S), jnp.int32),
            pltpu.SMEM((1, 1), jnp.int32),
            pltpu.SMEM((S,), jnp.int32), pltpu.SMEM((C * R,), jnp.int32), V((Z, Q, T // Q, F), F32),
            V((Z, Q, T // Q, F), BF16), V((Z, Q, T // Q, F), BF16), V((Z, Q, T // Q, F), BF16),
            V((2, Z, Q, T // Q, F), BF16),
            V((T, F), BF16), V((T, F), BF16), V((T, F), BF16), V((C, Q, F, T // Q), BF16), V((R, F, T), F32),
            V((Ro, F, T), BF16), V((Ro, F, T), BF16), V((Ro, F, T), BF16), V((Ro, F, T), BF16),
            V((T, F), BF16),
            V((F, F), BF16), V((C, H, F), BF16), V((R, H, F), BF16), V((F, F), BF16),
            V((F, F), F32),
            dma((10,)), dma((2 * Ro,)), dma((R,)), dma((Z, Q)), dma((Z, Q)), dma((Z, Q)),
            dma((2, Z, Q)), dma((3, Z, Q)), dma((C, Q)), dma((Ro,)), dma((Ro,)), dma((Ro,)), dma((Ro,)),
            dma((C,)), dma((C,)), dma((R,)), dma((R,)), dma((C,)), dma((C,)),
        ],
        compiler_params=pltpu.CompilerParams(
            collective_id=0, has_side_effects=True, vmem_limit_bytes=62 * 1024 * 1024,
        ),
        cost_estimate=pl.CostEstimate(
            flops=4 * C * R * T * T * F, bytes_accessed=2 * S * T * T, transcendentals=T * F),
    )(features, adj_tiles, tile_rows, tile_cols, tile_count, weight, grad_out)
    return pl.pallas_call(
        hand_out,
        out_shape=tuple(jax.ShapeDtypeStruct(o.shape, o.dtype) for o in outs),
        in_specs=[any_space] * 3,
        out_specs=(hbm,) * 3,
        scratch_shapes=[V(o.shape, o.dtype) for o in outs] + [dma((6,))],
        compiler_params=pltpu.CompilerParams(vmem_limit_bytes=62 * 1024 * 1024),
    )(*outs)


def solution(mesh):
    return jax.shard_map(
        local,
        mesh=mesh,
        in_specs=(
            P(("col", "row"), None),
            P("row", "col", None, None, None),
            P("row", "col", None),
            P("row", "col", None),
            P("row", "col"),
            P(),
            P(("row", "col"), None),
        ),
        out_specs=(P(("row", "col"), None), P(), P(("col", "row"), None)),
        check_vma=False,
    )
```

```python
import functools
import math

import jax
import jax.numpy as jnp
from jax import lax
from jax.experimental import pallas as pl
from jax.experimental.pallas import tpu as pltpu
from jax.sharding import PartitionSpec as P

MESH = pl.DeviceIdType.MESH
BF16 = jnp.bfloat16
F32 = jnp.float32
Q = 2


def dot(a, b):
    return jnp.dot(a, b, preferred_element_type=F32)


def kernel(
    R, C, S, T, F, scale,
    feat, adj, trow, tcol, tcnt, wt, gout,
    act_out, wg_out, xg_out,
    tiles, xs, wv, gv, rows_s, cols_s, cnt_s, pos, inv, accf,
    xsend, xrecv, zsend, zrecv, actv, aggv, gradv, mt, bacc,
    bsend, brecv, osend, orecv, xgv,
    wterm, wr1, wr2, wr3, wgv,
    loc, fs, fr, ps, pr, zs, zr, ms, mr, bs, br, os_, or_,
    w1s, w1r, w2s, w2r, w3s, w3r,
):
    r = lax.axis_index("row")
    c = lax.axis_index("col")
    Ro, Z = R // 2, C // 2
    yo, k = r // 2, r % 2
    z, x = c // 2, c % 2
    inner = yo * 2 + 1 - k
    xpeer = z * 2 + 1 - x
    H = T // C

    def remote(src, dst, ss, rs, row, col):
        return pltpu.make_async_remote_copy(
            src_ref=src, dst_ref=dst, send_sem=ss, recv_sem=rs,
            device_id={"row": row, "col": col}, device_id_type=MESH,
        )

    def arrived(dst, rs):
        pltpu.make_async_copy(dst, dst, rs).wait()

    c_feat = pltpu.make_async_copy(feat, xs.at[r], loc.at[0])
    c_feat.start()
    c_adj = pltpu.make_async_copy(adj.at[0, 0], tiles.at[pl.ds(0, S)], loc.at[1])
    c_adj.start()
    c_w = pltpu.make_async_copy(wt, wv, loc.at[2])
    c_w.start()
    c_g = pltpu.make_async_copy(gout, gv, loc.at[3])
    c_g.start()

    c_ids = [
        pltpu.make_async_copy(src, dst, loc.at[7 + n])
        for n, (src, dst) in enumerate(((trow, rows_s), (tcol, cols_s), (tcnt, cnt_s)))
    ]
    for cp in c_ids:
        cp.start()

    barrier = pltpu.get_barrier_semaphore()
    for o in range(1, R):
        pl.semaphore_signal(
            barrier, inc=1, device_id={"row": (r + o) % R, "col": c}, device_id_type=MESH)
    for o in range(1, C):
        pl.semaphore_signal(
            barrier, inc=1, device_id={"row": r, "col": (c + o) % C}, device_id_type=MESH)
    pl.semaphore_wait(barrier, R - 1 + C - 1)

    c_feat.wait()
    fcopies = []
    for o in range(1, Ro):
        cp = remote(xs.at[r], xs.at[r], fs.at[o], fr.at[r], ((yo + o) % Ro) * 2 + k, c)
        cp.start()
        fcopies.append(cp)
    cp = remote(xs.at[r], xs.at[r], fs.at[0], fr.at[r], inner, c)
    cp.start()
    fcopies.append(cp)

    tiles[S] = jnp.zeros((T, T), BF16)
    for cp in c_ids:
        cp.wait()
    total = cnt_s[0, 0]

    def set_pos(s, _):
        pos[s] = jnp.where(s < total, rows_s[0, 0, s] * R + cols_s[0, 0, s], -1)
        return 0

    lax.fori_loop(0, S, set_pos, 0)

    def set_inv(p, _):
        slot = jnp.int32(S)
        for s in range(S):
            slot = jnp.where(pos[s] == p, jnp.int32(s), slot)
        inv[p] = slot
        return 0

    lax.fori_loop(0, C * R, set_inv, 0)

    for o in range(1, Ro):
        j = ((yo - o + Ro) % Ro) * 2 + k
        arrived(xs.at[j], fr.at[j])
        cp = remote(xs.at[j], xs.at[j], fs.at[Ro - 1 + o], fr.at[j], inner, c)
        cp.start()
        fcopies.append(cp)
    arrived(xs.at[inner], fr.at[inner])
    c_adj.wait()
    for o in range(1, Ro):
        j = ((yo - o + Ro) % Ro) * 2 + 1 - k
        arrived(xs.at[j], fr.at[j])

    tables = [sorted(range(Z), key=lambda d, zz=zz: (-abs(d - zz), d)) for zz in range(Z)]
    order = []
    for kk in range(Z):
        v = jnp.int32(tables[0][kk])
        for zz in range(1, Z):
            v = jnp.where(z == zz, jnp.int32(tables[zz][kk]), v)
        order.append(v)

    def pick(n):
        v = order[0]
        for kk in range(1, Z):
            v = jnp.where(n == kk, order[kk], v)
        return v

    def partial(i):
        row = jnp.concatenate([tiles[inv[i * R + j]] for j in range(R)], axis=1)
        return dot(row, xs[...].reshape(R * T, F))

    def px(n, q):
        return remote(xsend.at[n, q], xrecv.at[n, q], ps.at[n, q], pr.at[n, q], r, xpeer)

    def fwd_peer(n, _):
        xsend[n] = partial(pick(n) * 2 + 1 - x).astype(BF16).reshape(Q, T // Q, F)
        px(n, 0).start()
        return 0

    lax.fori_loop(0, Z, fwd_peer, 0)

    def fwd_later(m, _):
        px(m % Z, m // Z).start()
        return 0

    lax.fori_loop(Z, Q * Z, fwd_later, 0)

    def pz(n, d, q):
        return remote(zsend.at[n, q], zrecv.at[z, q], zs.at[n, q], zr.at[z, q], r, d * 2 + x)

    def piece(n, q):
        arrived(xrecv.at[n, q], pr.at[n, q])
        zsend[n, q] = (accf[n, q] + xrecv[n, q].astype(F32)).astype(BF16)
        pz(n, pick(n), q).start()

    def last_piece(q):
        arrived(xrecv.at[Z - 1, q], pr.at[Z - 1, q])
        total = accf[Z - 1, q] + xrecv[Z - 1, q].astype(F32)
        for o in range(1, Z):
            src = (z + o) % Z
            arrived(zrecv.at[src, q], zr.at[src, q])
            total += zrecv[src, q].astype(F32)
        return total

    def fwd_chain(m, _):
        q, n = m // Z, m % Z

        @pl.when(q == 0)
        def _():
            accf[n] = partial(pick(n) * 2 + x).reshape(Q, T // Q, F)

        @pl.when(n < Z - 1)
        def _():
            piece(n, q)

        return 0

    lax.fori_loop(0, Q * Z, fwd_chain, 0)

    def to_z(n, q):
        return remote(mt.at[c, q], mt.at[c, q], ms.at[0, n, q], mr.at[c, q], r,
                      pick(Z - 1 - n) * 2 + x)

    def to_peer(n, q):
        i = pick(Z - 1 - n) * 2 + x
        return remote(mt.at[i, q], mt.at[i, q], ms.at[1, n, q], mr.at[i, q], r, xpeer)

    c_w.wait()
    c_g.wait()

    def dense(q, _):
        rows = pl.ds(pl.multiple_of(q * (T // Q), T // Q), T // Q)
        agg = last_piece(q).astype(BF16)
        pre = dot(agg, wv[...])
        sig = jax.nn.sigmoid(pre)
        grad = (gv[rows, :].astype(F32) * sig * (1.0 + pre * (1.0 - sig))).astype(BF16)
        mt[c, q] = lax.dot_general(
            wv[...], grad, (((1,), (1,)), ((), ())), preferred_element_type=F32).astype(BF16)
        to_peer(0, q).start()
        for n in range(1, Z):
            to_z(n, q).start()
        aggv[rows, :] = agg
        gradv[rows, :] = grad
        actv[rows, :] = (pre * sig).astype(BF16)
        return 0

    lax.fori_loop(0, Q, dense, 0)
    c_act = pltpu.make_async_copy(actv, act_out, loc.at[4])
    c_act.start()

    def to_row(o):
        to = (c + o) % C
        return remote(wterm.at[pl.ds(pl.multiple_of(to * H, H), H)], wr1.at[o], w1s.at[o],
                      w1r.at[o], r, to)

    def add_blocks(blocks, first):
        left = jnp.concatenate([mt[i, q] for i, q in blocks], axis=1)
        for j in range(R):
            right = jnp.concatenate(
                [
                    tiles[inv[i * R + j], pl.ds(pl.multiple_of(q * (T // Q), T // Q), T // Q), :]
                    for i, q in blocks
                ],
                axis=0,
            )
            if first:
                bacc[j] = dot(left, right)
            else:
                bacc[j] += dot(left, right)

    def block_of(m, side):
        return pick(Z - 1 - m % Z) * 2 + side, m // Z

    add_blocks([(c, 0)], True)

    def bwd_step(m, _):
        zi, zq = block_of(m, x)

        @pl.when(m % Z > 0)
        def _():
            arrived(mt.at[zi, zq], mr.at[zi, zq])
            to_peer(m % Z, zq).start()

        xi, xq = block_of(m - 1, 1 - x)
        arrived(mt.at[xi, xq], mr.at[xi, xq])
        add_blocks([(zi, zq), (xi, xq)], False)

        @pl.when(m == 1)
        def _():
            aggt = jnp.transpose(aggv[...].astype(F32)).astype(BF16)
            wterm[...] = dot(aggt, gradv[...]).astype(BF16)
            for o in range(1, C):
                to_row(o).start()

        @pl.when(m == Q * Z - 1)
        def _():
            sel = wterm[pl.ds(pl.multiple_of(c * H, H), H), :].astype(F32)
            for o in range(1, C):
                arrived(wr1.at[o], w1r.at[o])
                sel += wr1[o].astype(F32)
            wr2[r] = sel.astype(BF16)
            for o in range(1, R):
                remote(wr2.at[r], wr2.at[r], w2s.at[o], w2r.at[r], (r + o) % R, c).start()

        return 0

    lax.fori_loop(1, Q * Z, bwd_step, 0)
    xi, xq = block_of(Q * Z - 1, 1 - x)
    arrived(mt.at[xi, xq], mr.at[xi, xq])
    add_blocks([(xi, xq)], False)

    def bx(o):
        to = (yo + o) % Ro
        return remote(bsend.at[o], brecv.at[o], bs.at[o], br.at[o], r - r % 2 + 1 - k, c)

    for o in list(range(1, Ro)) + [0]:
        to = (yo + o) % Ro
        bsend[o] = bacc[to * 2 + 1 - k].astype(BF16)
        bx(o).start()
    bcopies = []
    for o in range(1, Ro):
        to = (yo + o) % Ro
        arrived(brecv.at[o], br.at[o])
        osend[o] = (bacc[to * 2 + k] + brecv[o].astype(F32)).astype(BF16)
        cp = remote(osend.at[o], orecv.at[o], os_.at[o], or_.at[o], to * 2 + k, c)
        cp.start()
        bcopies.append(cp)

    for o in range(1, R):
        arrived(wr2.at[(r + o) % R], w2r.at[(r + o) % R])
    sel = wr2[0].astype(F32)
    for j in range(1, R):
        sel += wr2[j].astype(F32)
    wr3[pl.ds(pl.multiple_of(c * H, H), H), :] = (sel * scale).astype(BF16)
    mine = wr3.at[pl.ds(pl.multiple_of(c * H, H), H)]
    w3copies = []
    for o in range(1, C):
        cp = remote(mine, mine, w3s.at[o], w3r.at[c], r, (c + o) % C)
        cp.start()
        w3copies.append(cp)

    arrived(brecv.at[0], br.at[0])
    xg = bacc[r] + brecv[0].astype(F32)
    for o in range(1, Ro):
        arrived(orecv.at[o], or_.at[o])
        xg += orecv[o].astype(F32)
    xgv[...] = jnp.transpose(xg).astype(BF16)
    c_xg = pltpu.make_async_copy(xgv, xg_out, loc.at[5])
    c_xg.start()

    for o in range(1, C):
        src = (c + o) % C
        arrived(wr3.at[pl.ds(pl.multiple_of(src * H, H), H)], w3r.at[src])
    wgv[...] = wr3[...].astype(F32)
    c_wg = pltpu.make_async_copy(wgv, wg_out, loc.at[6])
    c_wg.start()

    for cp in fcopies:
        cp.wait_send()

    def sent(n, _):
        for q in range(Q):
            px(n, q).wait_send()
            to_peer(n, q).wait_send()

            @pl.when(n > 0)
            def _():
                pz(n - 1, pick(n - 1), q).wait_send()
                to_z(n, q).wait_send()

        return 0

    lax.fori_loop(0, Z, sent, 0)
    for o in range(1, C):
        to_row(o).wait_send()
    for cp in w3copies + bcopies:
        cp.wait_send()
    for o in range(1, R):
        remote(wr2.at[r], wr2.at[r], w2s.at[o], w2r.at[r], (r + o) % R, c).wait_send()
    for o in range(Ro):
        bx(o).wait_send()
    c_act.wait()
    c_xg.wait()
    c_wg.wait()


def hand_out(*refs):
    held, sems = refs[6:9], refs[9]
    come = [pltpu.make_async_copy(refs[n], held[n], sems.at[n]) for n in range(3)]
    go = [pltpu.make_async_copy(held[n], refs[3 + n], sems.at[3 + n]) for n in range(3)]
    for cp in come:
        cp.start()
    for n in range(3):
        come[n].wait()
        go[n].start()
    for cp in go:
        cp.wait()


def local(features, adj_tiles, tile_rows, tile_cols, tile_count, weight, grad_out):
    R, C = lax.axis_size("row"), lax.axis_size("col")
    S, T = adj_tiles.shape[2], adj_tiles.shape[3]
    B, F = features.shape
    assert B == T and R % 2 == 0 and C % 2 == 0 and T % (16 * C) == 0
    Ro, Z = R // 2, C // 2
    H = T // C
    hbm = pl.BlockSpec(memory_space=pltpu.HBM)
    any_space = pl.BlockSpec(memory_space=pl.ANY)
    V = pltpu.VMEM
    dma = pltpu.SemaphoreType.DMA
    outs = pl.pallas_call(
        functools.partial(kernel, R, C, S, T, F, 1.0 / math.sqrt(B * R * C)),
        out_shape=(
            jax.ShapeDtypeStruct((B, F), BF16),
            jax.ShapeDtypeStruct((F, F), F32),
            jax.ShapeDtypeStruct((B, F), BF16),
        ),
        in_specs=[hbm] * 7,
        out_specs=(any_space, any_space, any_space),
        scratch_shapes=[
            V((S + 1, T, T), BF16), V((R, T, F), BF16), V((F, F), BF16), V((T, F), BF16),
            pltpu.SMEM((1, 1, S), jnp.int32), pltpu.SMEM((1, 1, S), jnp.int32),
            pltpu.SMEM((1, 1), jnp.int32),
            pltpu.SMEM((S,), jnp.int32), pltpu.SMEM((C * R,), jnp.int32), V((Z, Q, T // Q, F), F32),
            V((Z, Q, T // Q, F), BF16), V((Z, Q, T // Q, F), BF16), V((Z, Q, T // Q, F), BF16),
            V((Z, Q, T // Q, F), BF16),
            V((T, F), BF16), V((T, F), BF16), V((T, F), BF16), V((C, Q, F, T // Q), BF16), V((R, F, T), F32),
            V((Ro, F, T), BF16), V((Ro, F, T), BF16), V((Ro, F, T), BF16), V((Ro, F, T), BF16),
            V((T, F), BF16),
            V((F, F), BF16), V((C, H, F), BF16), V((R, H, F), BF16), V((F, F), BF16),
            V((F, F), F32),
            dma((10,)), dma((2 * Ro,)), dma((R,)), dma((Z, Q)), dma((Z, Q)), dma((Z, Q)),
            dma((Z, Q)), dma((2, Z, Q)), dma((C, Q)), dma((Ro,)), dma((Ro,)), dma((Ro,)), dma((Ro,)),
            dma((C,)), dma((C,)), dma((R,)), dma((R,)), dma((C,)), dma((C,)),
        ],
        compiler_params=pltpu.CompilerParams(
            collective_id=0, has_side_effects=True, vmem_limit_bytes=62 * 1024 * 1024,
        ),
        cost_estimate=pl.CostEstimate(
            flops=4 * C * R * T * T * F, bytes_accessed=2 * S * T * T, transcendentals=T * F),
    )(features, adj_tiles, tile_rows, tile_cols, tile_count, weight, grad_out)
    return pl.pallas_call(
        hand_out,
        out_shape=tuple(jax.ShapeDtypeStruct(o.shape, o.dtype) for o in outs),
        in_specs=[any_space] * 3,
        out_specs=(hbm,) * 3,
        scratch_shapes=[V(o.shape, o.dtype) for o in outs] + [dma((6,))],
        compiler_params=pltpu.CompilerParams(vmem_limit_bytes=62 * 1024 * 1024),
    )(*outs)


def solution(mesh):
    return jax.shard_map(
        local,
        mesh=mesh,
        in_specs=(
            P(("col", "row"), None),
            P("row", "col", None, None, None),
            P("row", "col", None),
            P("row", "col", None),
            P("row", "col"),
            P(),
            P(("row", "col"), None),
        ),
        out_specs=(P(("row", "col"), None), P(), P(("col", "row"), None)),
        check_vma=False,
    )
```

```python
import functools
import math

import jax
import jax.numpy as jnp
from jax import lax
from jax.experimental import pallas as pl
from jax.experimental.pallas import tpu as pltpu
from jax.sharding import PartitionSpec as P

MESH = pl.DeviceIdType.MESH
BF16 = jnp.bfloat16
F32 = jnp.float32
Q = 2


def dot(a, b):
    return jnp.dot(a, b, preferred_element_type=F32)


def kernel(
    R, C, S, T, F, scale,
    feat, adj, trow, tcol, tcnt, wt, gout,
    act_out, wg_out, xg_out,
    tiles, xs, wv, gv, rows_s, cols_s, cnt_s, pos, inv, accf,
    xsend, xrecv, zsend, zrecv, actv, aggv, gradv, mt, bacc,
    bsend, brecv, osend, orecv, xgv,
    wterm, wr1, wr2, wr3, wgv,
    loc, fs, fr, ps, pr, zs, zr, ms, mr, bs, br, os_, or_,
    w1s, w1r, w2s, w2r, w3s, w3r,
):
    r = lax.axis_index("row")
    c = lax.axis_index("col")
    Ro, Z = R // 2, C // 2
    yo, k = r // 2, r % 2
    z, x = c // 2, c % 2
    inner = yo * 2 + 1 - k
    xpeer = z * 2 + 1 - x
    H = T // C

    def remote(src, dst, ss, rs, row, col):
        return pltpu.make_async_remote_copy(
            src_ref=src, dst_ref=dst, send_sem=ss, recv_sem=rs,
            device_id={"row": row, "col": col}, device_id_type=MESH,
        )

    def arrived(dst, rs):
        pltpu.make_async_copy(dst, dst, rs).wait()

    c_feat = pltpu.make_async_copy(feat, xs.at[r], loc.at[0])
    c_feat.start()
    c_adj = pltpu.make_async_copy(adj.at[0, 0], tiles.at[pl.ds(0, S)], loc.at[1])
    c_adj.start()
    c_w = pltpu.make_async_copy(wt, wv, loc.at[2])
    c_w.start()
    c_g = pltpu.make_async_copy(gout, gv, loc.at[3])
    c_g.start()

    c_ids = [
        pltpu.make_async_copy(src, dst, loc.at[7 + n])
        for n, (src, dst) in enumerate(((trow, rows_s), (tcol, cols_s), (tcnt, cnt_s)))
    ]
    for cp in c_ids:
        cp.start()

    barrier = pltpu.get_barrier_semaphore()
    for o in range(1, R):
        pl.semaphore_signal(
            barrier, inc=1, device_id={"row": (r + o) % R, "col": c}, device_id_type=MESH)
    for o in range(1, C):
        pl.semaphore_signal(
            barrier, inc=1, device_id={"row": r, "col": (c + o) % C}, device_id_type=MESH)
    pl.semaphore_wait(barrier, R - 1 + C - 1)

    c_feat.wait()
    fcopies = []
    for o in range(1, Ro):
        cp = remote(xs.at[r], xs.at[r], fs.at[o], fr.at[r], ((yo + o) % Ro) * 2 + k, c)
        cp.start()
        fcopies.append(cp)
    cp = remote(xs.at[r], xs.at[r], fs.at[0], fr.at[r], inner, c)
    cp.start()
    fcopies.append(cp)

    tiles[S] = jnp.zeros((T, T), BF16)
    for cp in c_ids:
        cp.wait()
    total = cnt_s[0, 0]

    def set_pos(s, _):
        pos[s] = jnp.where(s < total, rows_s[0, 0, s] * R + cols_s[0, 0, s], -1)
        return 0

    lax.fori_loop(0, S, set_pos, 0)

    def set_inv(p, _):
        slot = jnp.int32(S)
        for s in range(S):
            slot = jnp.where(pos[s] == p, jnp.int32(s), slot)
        inv[p] = slot
        return 0

    lax.fori_loop(0, C * R, set_inv, 0)

    for o in range(1, Ro):
        j = ((yo - o + Ro) % Ro) * 2 + k
        arrived(xs.at[j], fr.at[j])
        cp = remote(xs.at[j], xs.at[j], fs.at[Ro - 1 + o], fr.at[j], inner, c)
        cp.start()
        fcopies.append(cp)
    arrived(xs.at[inner], fr.at[inner])
    c_adj.wait()
    for o in range(1, Ro):
        j = ((yo - o + Ro) % Ro) * 2 + 1 - k
        arrived(xs.at[j], fr.at[j])

    tables = [sorted(range(Z), key=lambda d, zz=zz: (-abs(d - zz), d)) for zz in range(Z)]
    order = []
    for kk in range(Z):
        v = jnp.int32(tables[0][kk])
        for zz in range(1, Z):
            v = jnp.where(z == zz, jnp.int32(tables[zz][kk]), v)
        order.append(v)

    def pick(n):
        v = order[0]
        for kk in range(1, Z):
            v = jnp.where(n == kk, order[kk], v)
        return v

    def partial(i):
        row = jnp.concatenate([tiles[inv[i * R + j]] for j in range(R)], axis=1)
        return dot(row, xs[...].reshape(R * T, F))

    def px(n, q):
        return remote(xsend.at[n, q], xrecv.at[n, q], ps.at[n, q], pr.at[n, q], r, xpeer)

    def fwd_peer(n, _):
        xsend[n] = partial(pick(n) * 2 + 1 - x).astype(BF16).reshape(Q, T // Q, F)

        @pl.when(n == 0)
        def _():
            for q in range(Q):
                px(0, q).start()

        return 0

    lax.fori_loop(0, Z, fwd_peer, 0)

    def pz(n, d, q):
        right = d > z
        way = jnp.where(right, 0, 1)
        nxt = jnp.where(right, z + 1, z - 1)
        return remote(zsend.at[n, q], zrecv.at[way, d, q], zs.at[n, q], zr.at[way, d, q], r,
                      nxt * 2 + x)

    def fwd_chain(n, _):
        d = pick(n)
        accf[...] = partial(d * 2 + x).reshape(Q, T // Q, F)

        def piece(q, _):
            px(n, q).wait_send()

            @pl.when(n < Z - 1)
            def _():
                px(n + 1, q).start()

            arrived(xrecv.at[n, q], pr.at[n, q])
            accf[q] += xrecv[n, q].astype(F32)

            @pl.when((d >= z) & (z > 0))
            def _():
                arrived(zrecv.at[0, d, q], zr.at[0, d, q])
                accf[q] += zrecv[0, d, q].astype(F32)

            @pl.when((d <= z) & (z < Z - 1))
            def _():
                arrived(zrecv.at[1, d, q], zr.at[1, d, q])
                accf[q] += zrecv[1, d, q].astype(F32)

            @pl.when(d != z)
            def _():
                zsend[n, q] = accf[q].astype(BF16)
                pz(n, d, q).start()

            return 0

        lax.fori_loop(0, Q, piece, 0)
        return 0

    lax.fori_loop(0, Z, fwd_chain, 0)

    c_w.wait()
    c_g.wait()
    agg = accf[...].reshape(T, F).astype(BF16)
    pre = dot(agg, wv[...])
    sig = jax.nn.sigmoid(pre)
    grad = (gv[...].astype(F32) * sig * (1.0 + pre * (1.0 - sig))).astype(BF16)
    mt[c] = lax.dot_general(
        wv[...], grad, (((1,), (1,)), ((), ())), preferred_element_type=F32
    ).astype(BF16).reshape(Q, F // Q, T)

    def to_z(n, s, q, way):
        i = s * 2 + x
        return remote(mt.at[i, q], mt.at[i, q], ms.at[way, n, q], mr.at[i, q], r,
                      (z + 1 - 2 * way) * 2 + x)

    def to_peer(n, s, q):
        i = s * 2 + x
        return remote(mt.at[i, q], mt.at[i, q], ms.at[2, n, q], mr.at[i, q], r, xpeer)

    def spread(n, s, q, act):
        @pl.when((s <= z) & (z < Z - 1))
        def _():
            act(to_z(n, s, q, 0))

        @pl.when((s >= z) & (z > 0))
        def _():
            act(to_z(n, s, q, 1))

        act(to_peer(n, s, q))

    for q in range(Q):
        spread(0, z, q, lambda cp: cp.start())

    aggv[...] = agg
    gradv[...] = grad
    actv[...] = (pre * sig).astype(BF16)
    c_act = pltpu.make_async_copy(actv, act_out, loc.at[4])
    c_act.start()

    def to_row(o):
        to = (c + o) % C
        return remote(wterm.at[pl.ds(pl.multiple_of(to * H, H), H)], wr1.at[o], w1s.at[o],
                      w1r.at[o], r, to)

    def add_blocks(blocks, first):
        left = jnp.concatenate([mt[i].reshape(F, T) for i in blocks], axis=1)
        for j in range(R):
            right = jnp.concatenate([tiles[inv[i * R + j]] for i in blocks], axis=0)
            if first:
                bacc[j] = dot(left, right)
            else:
                bacc[j] += dot(left, right)

    add_blocks([c], True)

    def bwd_step(m, _):
        s = pick(Z - 1 - m)
        zi = s * 2 + x
        for q in range(Q):
            arrived(mt.at[zi, q], mr.at[zi, q])
            spread(m, s, q, lambda cp: cp.start())
        xi = pick(Z - m) * 2 + 1 - x
        for q in range(Q):
            arrived(mt.at[xi, q], mr.at[xi, q])
        add_blocks([zi, xi], False)

        @pl.when(m == 1)
        def _():
            aggt = jnp.transpose(aggv[...].astype(F32)).astype(BF16)
            wterm[...] = dot(aggt, gradv[...]).astype(BF16)
            for o in range(1, C):
                to_row(o).start()

        @pl.when(m == Z - 1)
        def _():
            sel = wterm[pl.ds(pl.multiple_of(c * H, H), H), :].astype(F32)
            for o in range(1, C):
                arrived(wr1.at[o], w1r.at[o])
                sel += wr1[o].astype(F32)
            wr2[r] = sel.astype(BF16)
            for o in range(1, R):
                remote(wr2.at[r], wr2.at[r], w2s.at[o], w2r.at[r], (r + o) % R, c).start()

        return 0

    lax.fori_loop(1, Z, bwd_step, 0)
    xi = pick(0) * 2 + 1 - x
    for q in range(Q):
        arrived(mt.at[xi, q], mr.at[xi, q])
    add_blocks([xi], False)

    def bx(o):
        to = (yo + o) % Ro
        return remote(bsend.at[o], brecv.at[o], bs.at[o], br.at[o], r - r % 2 + 1 - k, c)

    for o in list(range(1, Ro)) + [0]:
        to = (yo + o) % Ro
        bsend[o] = bacc[to * 2 + 1 - k].astype(BF16)
        bx(o).start()
    bcopies = []
    for o in range(1, Ro):
        to = (yo + o) % Ro
        arrived(brecv.at[o], br.at[o])
        osend[o] = (bacc[to * 2 + k] + brecv[o].astype(F32)).astype(BF16)
        cp = remote(osend.at[o], orecv.at[o], os_.at[o], or_.at[o], to * 2 + k, c)
        cp.start()
        bcopies.append(cp)

    for o in range(1, R):
        arrived(wr2.at[(r + o) % R], w2r.at[(r + o) % R])
    sel = wr2[0].astype(F32)
    for j in range(1, R):
        sel += wr2[j].astype(F32)
    wr3[pl.ds(pl.multiple_of(c * H, H), H), :] = (sel * scale).astype(BF16)
    mine = wr3.at[pl.ds(pl.multiple_of(c * H, H), H)]
    w3copies = []
    for o in range(1, C):
        cp = remote(mine, mine, w3s.at[o], w3r.at[c], r, (c + o) % C)
        cp.start()
        w3copies.append(cp)

    arrived(brecv.at[0], br.at[0])
    xg = bacc[r] + brecv[0].astype(F32)
    for o in range(1, Ro):
        arrived(orecv.at[o], or_.at[o])
        xg += orecv[o].astype(F32)
    xgv[...] = jnp.transpose(xg).astype(BF16)
    c_xg = pltpu.make_async_copy(xgv, xg_out, loc.at[5])
    c_xg.start()

    for o in range(1, C):
        src = (c + o) % C
        arrived(wr3.at[pl.ds(pl.multiple_of(src * H, H), H)], w3r.at[src])
    wgv[...] = wr3[...].astype(F32)
    c_wg = pltpu.make_async_copy(wgv, wg_out, loc.at[6])
    c_wg.start()

    for cp in fcopies:
        cp.wait_send()

    def sent(n, _):
        d = pick(n)
        for q in range(Q):
            @pl.when(d != z)
            def _():
                pz(n, d, q).wait_send()

            spread(n, pick(Z - 1 - n), q, lambda cp: cp.wait_send())

        return 0

    lax.fori_loop(0, Z, sent, 0)
    for o in range(1, C):
        to_row(o).wait_send()
    for cp in w3copies + bcopies:
        cp.wait_send()
    for o in range(1, R):
        remote(wr2.at[r], wr2.at[r], w2s.at[o], w2r.at[r], (r + o) % R, c).wait_send()
    for o in range(Ro):
        bx(o).wait_send()
    c_act.wait()
    c_xg.wait()
    c_wg.wait()


def hand_out(*refs):
    held, sems = refs[6:9], refs[9]
    come = [pltpu.make_async_copy(refs[n], held[n], sems.at[n]) for n in range(3)]
    go = [pltpu.make_async_copy(held[n], refs[3 + n], sems.at[3 + n]) for n in range(3)]
    for cp in come:
        cp.start()
    for n in range(3):
        come[n].wait()
        go[n].start()
    for cp in go:
        cp.wait()


def local(features, adj_tiles, tile_rows, tile_cols, tile_count, weight, grad_out):
    R, C = lax.axis_size("row"), lax.axis_size("col")
    S, T = adj_tiles.shape[2], adj_tiles.shape[3]
    B, F = features.shape
    assert B == T and R % 2 == 0 and C % 2 == 0 and T % (16 * C) == 0
    Ro, Z = R // 2, C // 2
    H = T // C
    hbm = pl.BlockSpec(memory_space=pltpu.HBM)
    any_space = pl.BlockSpec(memory_space=pl.ANY)
    V = pltpu.VMEM
    dma = pltpu.SemaphoreType.DMA
    outs = pl.pallas_call(
        functools.partial(kernel, R, C, S, T, F, 1.0 / math.sqrt(B * R * C)),
        out_shape=(
            jax.ShapeDtypeStruct((B, F), BF16),
            jax.ShapeDtypeStruct((F, F), F32),
            jax.ShapeDtypeStruct((B, F), BF16),
        ),
        in_specs=[hbm] * 7,
        out_specs=(any_space, any_space, any_space),
        scratch_shapes=[
            V((S + 1, T, T), BF16), V((R, T, F), BF16), V((F, F), BF16), V((T, F), BF16),
            pltpu.SMEM((1, 1, S), jnp.int32), pltpu.SMEM((1, 1, S), jnp.int32),
            pltpu.SMEM((1, 1), jnp.int32),
            pltpu.SMEM((S,), jnp.int32), pltpu.SMEM((C * R,), jnp.int32), V((Q, T // Q, F), F32),
            V((Z, Q, T // Q, F), BF16), V((Z, Q, T // Q, F), BF16), V((Z, Q, T // Q, F), BF16),
            V((2, Z, Q, T // Q, F), BF16),
            V((T, F), BF16), V((T, F), BF16), V((T, F), BF16), V((C, Q, F // Q, T), BF16), V((R, F, T), F32),
            V((Ro, F, T), BF16), V((Ro, F, T), BF16), V((Ro, F, T), BF16), V((Ro, F, T), BF16),
            V((T, F), BF16),
            V((F, F), BF16), V((C, H, F), BF16), V((R, H, F), BF16), V((F, F), BF16),
            V((F, F), F32),
            dma((10,)), dma((2 * Ro,)), dma((R,)), dma((Z, Q)), dma((Z, Q)), dma((Z, Q)),
            dma((2, Z, Q)), dma((3, Z, Q)), dma((C, Q)), dma((Ro,)), dma((Ro,)), dma((Ro,)), dma((Ro,)),
            dma((C,)), dma((C,)), dma((R,)), dma((R,)), dma((C,)), dma((C,)),
        ],
        compiler_params=pltpu.CompilerParams(
            collective_id=0, has_side_effects=True, vmem_limit_bytes=62 * 1024 * 1024,
        ),
        cost_estimate=pl.CostEstimate(
            flops=4 * C * R * T * T * F, bytes_accessed=2 * S * T * T, transcendentals=T * F),
    )(features, adj_tiles, tile_rows, tile_cols, tile_count, weight, grad_out)
    return pl.pallas_call(
        hand_out,
        out_shape=tuple(jax.ShapeDtypeStruct(o.shape, o.dtype) for o in outs),
        in_specs=[any_space] * 3,
        out_specs=(hbm,) * 3,
        scratch_shapes=[V(o.shape, o.dtype) for o in outs] + [dma((6,))],
        compiler_params=pltpu.CompilerParams(vmem_limit_bytes=62 * 1024 * 1024),
    )(*outs)


def solution(mesh):
    return jax.shard_map(
        local,
        mesh=mesh,
        in_specs=(
            P(("col", "row"), None),
            P("row", "col", None, None, None),
            P("row", "col", None),
            P("row", "col", None),
            P("row", "col"),
            P(),
            P(("row", "col"), None),
        ),
        out_specs=(P(("row", "col"), None), P(), P(("col", "row"), None)),
        check_vma=False,
    )
```

```python
import functools
import math

import jax
import jax.numpy as jnp
from jax import lax
from jax.experimental import pallas as pl
from jax.experimental.pallas import tpu as pltpu
from jax.sharding import PartitionSpec as P

MESH = pl.DeviceIdType.MESH
BF16 = jnp.bfloat16
F32 = jnp.float32
Q = 4


def dot(a, b):
    return jnp.dot(a, b, preferred_element_type=F32)


def kernel(
    R, C, S, T, F, scale,
    feat, adj, trow, tcol, tcnt, wt, gout,
    act_out, wg_out, xg_out,
    tiles, xs, wv, gv, rows_s, cols_s, cnt_s, pos, inv, accf,
    xsend, xrecv, zsend, zrecv, actv, aggv, gradv, mt, bacc,
    bsend, brecv, osend, orecv, xgv,
    wterm, wr1, wr2, wr3, wgv,
    loc, fs, fr, ps, pr, zs, zr, ms, mr, bs, br, os_, or_,
    w1s, w1r, w2s, w2r, w3s, w3r,
):
    r = lax.axis_index("row")
    c = lax.axis_index("col")
    Ro, Z = R // 2, C // 2
    yo, k = r // 2, r % 2
    z, x = c // 2, c % 2
    inner = yo * 2 + 1 - k
    xpeer = z * 2 + 1 - x
    H = T // C

    def remote(src, dst, ss, rs, row, col):
        return pltpu.make_async_remote_copy(
            src_ref=src, dst_ref=dst, send_sem=ss, recv_sem=rs,
            device_id={"row": row, "col": col}, device_id_type=MESH,
        )

    def arrived(dst, rs):
        pltpu.make_async_copy(dst, dst, rs).wait()

    c_feat = pltpu.make_async_copy(feat, xs.at[r], loc.at[0])
    c_feat.start()
    c_adj = pltpu.make_async_copy(adj.at[0, 0], tiles.at[pl.ds(0, S)], loc.at[1])
    c_adj.start()
    c_w = pltpu.make_async_copy(wt, wv, loc.at[2])
    c_w.start()
    c_g = pltpu.make_async_copy(gout, gv, loc.at[3])
    c_g.start()

    c_ids = [
        pltpu.make_async_copy(src, dst, loc.at[7 + n])
        for n, (src, dst) in enumerate(((trow, rows_s), (tcol, cols_s), (tcnt, cnt_s)))
    ]
    for cp in c_ids:
        cp.start()

    barrier = pltpu.get_barrier_semaphore()
    for o in range(1, R):
        pl.semaphore_signal(
            barrier, inc=1, device_id={"row": (r + o) % R, "col": c}, device_id_type=MESH)
    for o in range(1, C):
        pl.semaphore_signal(
            barrier, inc=1, device_id={"row": r, "col": (c + o) % C}, device_id_type=MESH)
    pl.semaphore_wait(barrier, R - 1 + C - 1)

    c_feat.wait()
    fcopies = []
    for o in range(1, Ro):
        cp = remote(xs.at[r], xs.at[r], fs.at[o], fr.at[r], ((yo + o) % Ro) * 2 + k, c)
        cp.start()
        fcopies.append(cp)
    cp = remote(xs.at[r], xs.at[r], fs.at[0], fr.at[r], inner, c)
    cp.start()
    fcopies.append(cp)

    tiles[S] = jnp.zeros((T, T), BF16)
    for cp in c_ids:
        cp.wait()
    total = cnt_s[0, 0]

    def set_pos(s, _):
        pos[s] = jnp.where(s < total, rows_s[0, 0, s] * R + cols_s[0, 0, s], -1)
        return 0

    lax.fori_loop(0, S, set_pos, 0)

    def set_inv(p, _):
        slot = jnp.int32(S)
        for s in range(S):
            slot = jnp.where(pos[s] == p, jnp.int32(s), slot)
        inv[p] = slot
        return 0

    lax.fori_loop(0, C * R, set_inv, 0)

    for o in range(1, Ro):
        j = ((yo - o + Ro) % Ro) * 2 + k
        arrived(xs.at[j], fr.at[j])
        cp = remote(xs.at[j], xs.at[j], fs.at[Ro - 1 + o], fr.at[j], inner, c)
        cp.start()
        fcopies.append(cp)
    arrived(xs.at[inner], fr.at[inner])
    c_adj.wait()
    for o in range(1, Ro):
        j = ((yo - o + Ro) % Ro) * 2 + 1 - k
        arrived(xs.at[j], fr.at[j])

    tables = [sorted(range(Z), key=lambda d, zz=zz: (-abs(d - zz), d)) for zz in range(Z)]
    order = []
    for kk in range(Z):
        v = jnp.int32(tables[0][kk])
        for zz in range(1, Z):
            v = jnp.where(z == zz, jnp.int32(tables[zz][kk]), v)
        order.append(v)

    def pick(n):
        v = order[0]
        for kk in range(1, Z):
            v = jnp.where(n == kk, order[kk], v)
        return v

    def partial(i):
        row = jnp.concatenate([tiles[inv[i * R + j]] for j in range(R)], axis=1)
        return dot(row, xs[...].reshape(R * T, F))

    def px(n, q):
        return remote(xsend.at[n, q], xrecv.at[n, q], ps.at[n, q], pr.at[n, q], r, xpeer)

    def fwd_peer(n, _):
        xsend[n] = partial(pick(n) * 2 + 1 - x).astype(BF16).reshape(Q, T // Q, F)

        @pl.when(n == 0)
        def _():
            for q in range(Q):
                px(0, q).start()

        return 0

    lax.fori_loop(0, Z, fwd_peer, 0)

    def pz(n, d, q):
        right = d > z
        way = jnp.where(right, 0, 1)
        nxt = jnp.where(right, z + 1, z - 1)
        return remote(zsend.at[n, q], zrecv.at[way, d, q], zs.at[n, q], zr.at[way, d, q], r,
                      nxt * 2 + x)

    def fwd_chain(n, _):
        d = pick(n)
        accf[...] = partial(d * 2 + x).reshape(Q, T // Q, F)

        def piece(q, _):
            px(n, q).wait_send()

            @pl.when(n < Z - 1)
            def _():
                px(n + 1, q).start()

            arrived(xrecv.at[n, q], pr.at[n, q])
            accf[q] += xrecv[n, q].astype(F32)

            @pl.when((d >= z) & (z > 0))
            def _():
                arrived(zrecv.at[0, d, q], zr.at[0, d, q])
                accf[q] += zrecv[0, d, q].astype(F32)

            @pl.when((d <= z) & (z < Z - 1))
            def _():
                arrived(zrecv.at[1, d, q], zr.at[1, d, q])
                accf[q] += zrecv[1, d, q].astype(F32)

            @pl.when(d != z)
            def _():
                zsend[n, q] = accf[q].astype(BF16)
                pz(n, d, q).start()

            return 0

        lax.fori_loop(0, Q, piece, 0)
        return 0

    lax.fori_loop(0, Z, fwd_chain, 0)

    c_w.wait()
    c_g.wait()
    agg = accf[...].reshape(T, F).astype(BF16)
    pre = dot(agg, wv[...])
    sig = jax.nn.sigmoid(pre)
    grad = (gv[...].astype(F32) * sig * (1.0 + pre * (1.0 - sig))).astype(BF16)
    mt[c] = lax.dot_general(
        wv[...], grad, (((1,), (1,)), ((), ())), preferred_element_type=F32
    ).astype(BF16).reshape(Q, F // Q, T)

    def to_z(n, s, q, way):
        i = s * 2 + x
        return remote(mt.at[i, q], mt.at[i, q], ms.at[way, n, q], mr.at[i, q], r,
                      (z + 1 - 2 * way) * 2 + x)

    def to_peer(n, s, q):
        i = s * 2 + x
        return remote(mt.at[i, q], mt.at[i, q], ms.at[2, n, q], mr.at[i, q], r, xpeer)

    def spread(n, s, q, act):
        @pl.when((s <= z) & (z < Z - 1))
        def _():
            act(to_z(n, s, q, 0))

        @pl.when((s >= z) & (z > 0))
        def _():
            act(to_z(n, s, q, 1))

        act(to_peer(n, s, q))

    for q in range(Q):
        spread(0, z, q, lambda cp: cp.start())

    aggv[...] = agg
    gradv[...] = grad
    actv[...] = (pre * sig).astype(BF16)
    c_act = pltpu.make_async_copy(actv, act_out, loc.at[4])
    c_act.start()

    def to_row(o):
        to = (c + o) % C
        return remote(wterm.at[pl.ds(pl.multiple_of(to * H, H), H)], wr1.at[o], w1s.at[o],
                      w1r.at[o], r, to)

    def add_blocks(blocks, first):
        left = jnp.concatenate([mt[i].reshape(F, T) for i in blocks], axis=1)
        for j in range(R):
            right = jnp.concatenate([tiles[inv[i * R + j]] for i in blocks], axis=0)
            if first:
                bacc[j] = dot(left, right)
            else:
                bacc[j] += dot(left, right)

    add_blocks([c], True)

    def bwd_step(m, _):
        s = pick(Z - 1 - m)
        zi = s * 2 + x
        for q in range(Q):
            arrived(mt.at[zi, q], mr.at[zi, q])
            spread(m, s, q, lambda cp: cp.start())
        xi = pick(Z - m) * 2 + 1 - x
        for q in range(Q):
            arrived(mt.at[xi, q], mr.at[xi, q])
        add_blocks([zi, xi], False)

        @pl.when(m == 1)
        def _():
            aggt = jnp.transpose(aggv[...].astype(F32)).astype(BF16)
            wterm[...] = dot(aggt, gradv[...]).astype(BF16)
            for o in range(1, C):
                to_row(o).start()

        @pl.when(m == Z - 1)
        def _():
            sel = wterm[pl.ds(pl.multiple_of(c * H, H), H), :].astype(F32)
            for o in range(1, C):
                arrived(wr1.at[o], w1r.at[o])
                sel += wr1[o].astype(F32)
            wr2[r] = sel.astype(BF16)
            for o in range(1, R):
                remote(wr2.at[r], wr2.at[r], w2s.at[o], w2r.at[r], (r + o) % R, c).start()

        return 0

    lax.fori_loop(1, Z, bwd_step, 0)
    xi = pick(0) * 2 + 1 - x
    for q in range(Q):
        arrived(mt.at[xi, q], mr.at[xi, q])
    add_blocks([xi], False)

    def bx(o):
        to = (yo + o) % Ro
        return remote(bsend.at[o], brecv.at[o], bs.at[o], br.at[o], r - r % 2 + 1 - k, c)

    for o in list(range(1, Ro)) + [0]:
        to = (yo + o) % Ro
        bsend[o] = bacc[to * 2 + 1 - k].astype(BF16)
        bx(o).start()
    bcopies = []
    for o in range(1, Ro):
        to = (yo + o) % Ro
        arrived(brecv.at[o], br.at[o])
        osend[o] = (bacc[to * 2 + k] + brecv[o].astype(F32)).astype(BF16)
        cp = remote(osend.at[o], orecv.at[o], os_.at[o], or_.at[o], to * 2 + k, c)
        cp.start()
        bcopies.append(cp)

    for o in range(1, R):
        arrived(wr2.at[(r + o) % R], w2r.at[(r + o) % R])
    sel = wr2[0].astype(F32)
    for j in range(1, R):
        sel += wr2[j].astype(F32)
    wr3[pl.ds(pl.multiple_of(c * H, H), H), :] = (sel * scale).astype(BF16)
    mine = wr3.at[pl.ds(pl.multiple_of(c * H, H), H)]
    w3copies = []
    for o in range(1, C):
        cp = remote(mine, mine, w3s.at[o], w3r.at[c], r, (c + o) % C)
        cp.start()
        w3copies.append(cp)

    arrived(brecv.at[0], br.at[0])
    xg = bacc[r] + brecv[0].astype(F32)
    for o in range(1, Ro):
        arrived(orecv.at[o], or_.at[o])
        xg += orecv[o].astype(F32)
    xgv[...] = jnp.transpose(xg).astype(BF16)
    c_xg = pltpu.make_async_copy(xgv, xg_out, loc.at[5])
    c_xg.start()

    for o in range(1, C):
        src = (c + o) % C
        arrived(wr3.at[pl.ds(pl.multiple_of(src * H, H), H)], w3r.at[src])
    wgv[...] = wr3[...].astype(F32)
    c_wg = pltpu.make_async_copy(wgv, wg_out, loc.at[6])
    c_wg.start()

    for cp in fcopies:
        cp.wait_send()

    def sent(n, _):
        d = pick(n)
        for q in range(Q):
            @pl.when(d != z)
            def _():
                pz(n, d, q).wait_send()

            spread(n, pick(Z - 1 - n), q, lambda cp: cp.wait_send())

        return 0

    lax.fori_loop(0, Z, sent, 0)
    for o in range(1, C):
        to_row(o).wait_send()
    for cp in w3copies + bcopies:
        cp.wait_send()
    for o in range(1, R):
        remote(wr2.at[r], wr2.at[r], w2s.at[o], w2r.at[r], (r + o) % R, c).wait_send()
    for o in range(Ro):
        bx(o).wait_send()
    c_act.wait()
    c_xg.wait()
    c_wg.wait()


def hand_out(*refs):
    held, sems = refs[6:9], refs[9]
    come = [pltpu.make_async_copy(refs[n], held[n], sems.at[n]) for n in range(3)]
    go = [pltpu.make_async_copy(held[n], refs[3 + n], sems.at[3 + n]) for n in range(3)]
    for cp in come:
        cp.start()
    for n in range(3):
        come[n].wait()
        go[n].start()
    for cp in go:
        cp.wait()


def local(features, adj_tiles, tile_rows, tile_cols, tile_count, weight, grad_out):
    R, C = lax.axis_size("row"), lax.axis_size("col")
    S, T = adj_tiles.shape[2], adj_tiles.shape[3]
    B, F = features.shape
    assert B == T and R % 2 == 0 and C % 2 == 0 and T % (16 * C) == 0
    Ro, Z = R // 2, C // 2
    H = T // C
    hbm = pl.BlockSpec(memory_space=pltpu.HBM)
    any_space = pl.BlockSpec(memory_space=pl.ANY)
    V = pltpu.VMEM
    dma = pltpu.SemaphoreType.DMA
    outs = pl.pallas_call(
        functools.partial(kernel, R, C, S, T, F, 1.0 / math.sqrt(B * R * C)),
        out_shape=(
            jax.ShapeDtypeStruct((B, F), BF16),
            jax.ShapeDtypeStruct((F, F), F32),
            jax.ShapeDtypeStruct((B, F), BF16),
        ),
        in_specs=[hbm] * 7,
        out_specs=(any_space, any_space, any_space),
        scratch_shapes=[
            V((S + 1, T, T), BF16), V((R, T, F), BF16), V((F, F), BF16), V((T, F), BF16),
            pltpu.SMEM((1, 1, S), jnp.int32), pltpu.SMEM((1, 1, S), jnp.int32),
            pltpu.SMEM((1, 1), jnp.int32),
            pltpu.SMEM((S,), jnp.int32), pltpu.SMEM((C * R,), jnp.int32), V((Q, T // Q, F), F32),
            V((Z, Q, T // Q, F), BF16), V((Z, Q, T // Q, F), BF16), V((Z, Q, T // Q, F), BF16),
            V((2, Z, Q, T // Q, F), BF16),
            V((T, F), BF16), V((T, F), BF16), V((T, F), BF16), V((C, Q, F // Q, T), BF16), V((R, F, T), F32),
            V((Ro, F, T), BF16), V((Ro, F, T), BF16), V((Ro, F, T), BF16), V((Ro, F, T), BF16),
            V((T, F), BF16),
            V((F, F), BF16), V((C, H, F), BF16), V((R, H, F), BF16), V((F, F), BF16),
            V((F, F), F32),
            dma((10,)), dma((2 * Ro,)), dma((R,)), dma((Z, Q)), dma((Z, Q)), dma((Z, Q)),
            dma((2, Z, Q)), dma((3, Z, Q)), dma((C, Q)), dma((Ro,)), dma((Ro,)), dma((Ro,)), dma((Ro,)),
            dma((C,)), dma((C,)), dma((R,)), dma((R,)), dma((C,)), dma((C,)),
        ],
        compiler_params=pltpu.CompilerParams(
            collective_id=0, has_side_effects=True, vmem_limit_bytes=62 * 1024 * 1024,
        ),
        cost_estimate=pl.CostEstimate(
            flops=4 * C * R * T * T * F, bytes_accessed=2 * S * T * T, transcendentals=T * F),
    )(features, adj_tiles, tile_rows, tile_cols, tile_count, weight, grad_out)
    return pl.pallas_call(
        hand_out,
        out_shape=tuple(jax.ShapeDtypeStruct(o.shape, o.dtype) for o in outs),
        in_specs=[any_space] * 3,
        out_specs=(hbm,) * 3,
        scratch_shapes=[V(o.shape, o.dtype) for o in outs] + [dma((6,))],
        compiler_params=pltpu.CompilerParams(vmem_limit_bytes=62 * 1024 * 1024),
    )(*outs)


def solution(mesh):
    return jax.shard_map(
        local,
        mesh=mesh,
        in_specs=(
            P(("col", "row"), None),
            P("row", "col", None, None, None),
            P("row", "col", None),
            P("row", "col", None),
            P("row", "col"),
            P(),
            P(("row", "col"), None),
        ),
        out_specs=(P(("row", "col"), None), P(), P(("col", "row"), None)),
        check_vma=False,
    )
```

```python
import functools
import math

import jax
import jax.numpy as jnp
from jax import lax
from jax.experimental import pallas as pl
from jax.experimental.pallas import tpu as pltpu
from jax.sharding import PartitionSpec as P

MESH = pl.DeviceIdType.MESH
BF16 = jnp.bfloat16
F32 = jnp.float32
Q = 2


def dot(a, b):
    return jnp.dot(a, b, preferred_element_type=F32)


def kernel(
    R, C, S, T, F, scale,
    feat, adj, trow, tcol, tcnt, wt, gout,
    act_out, wg_out, xg_out,
    tiles, xs, wv, gv, rows_s, cols_s, cnt_s, pos, inv, accf,
    xsend, xrecv, xside, zsend, zrecv, actv, aggv, gradv, mt, bacc,
    bsend, brecv, osend, orecv, xgv,
    wterm, wr1, wr2, wr3, wgv,
    loc, fs, fr, ps, pr, zs, zr, ms, mr, bs, br, os_, or_,
    w1s, w1r, w2s, w2r, w3s, w3r,
):
    r = lax.axis_index("row")
    c = lax.axis_index("col")
    Ro, Z = R // 2, C // 2
    yo, k = r // 2, r % 2
    z, x = c // 2, c % 2
    inner = yo * 2 + 1 - k
    xpeer = z * 2 + 1 - x
    H = T // C

    def remote(src, dst, ss, rs, row, col):
        return pltpu.make_async_remote_copy(
            src_ref=src, dst_ref=dst, send_sem=ss, recv_sem=rs,
            device_id={"row": row, "col": col}, device_id_type=MESH,
        )

    def arrived(dst, rs):
        pltpu.make_async_copy(dst, dst, rs).wait()

    c_feat = pltpu.make_async_copy(feat, xs.at[r], loc.at[0])
    c_feat.start()
    c_adj = pltpu.make_async_copy(adj.at[0, 0], tiles.at[pl.ds(0, S)], loc.at[1])
    c_adj.start()
    c_w = pltpu.make_async_copy(wt, wv, loc.at[2])
    c_w.start()
    c_g = pltpu.make_async_copy(gout, gv, loc.at[3])
    c_g.start()

    c_ids = [
        pltpu.make_async_copy(src, dst, loc.at[7 + n])
        for n, (src, dst) in enumerate(((trow, rows_s), (tcol, cols_s), (tcnt, cnt_s)))
    ]
    for cp in c_ids:
        cp.start()

    barrier = pltpu.get_barrier_semaphore()
    for o in range(1, R):
        pl.semaphore_signal(
            barrier, inc=1, device_id={"row": (r + o) % R, "col": c}, device_id_type=MESH)
    for o in range(1, C):
        pl.semaphore_signal(
            barrier, inc=1, device_id={"row": r, "col": (c + o) % C}, device_id_type=MESH)
    pl.semaphore_wait(barrier, R - 1 + C - 1)

    c_feat.wait()
    fcopies = []
    for o in range(1, Ro):
        cp = remote(xs.at[r], xs.at[r], fs.at[o], fr.at[r], ((yo + o) % Ro) * 2 + k, c)
        cp.start()
        fcopies.append(cp)
    cp = remote(xs.at[r], xs.at[r], fs.at[0], fr.at[r], inner, c)
    cp.start()
    fcopies.append(cp)

    tiles[S] = jnp.zeros((T, T), BF16)
    for cp in c_ids:
        cp.wait()
    total = cnt_s[0, 0]

    def set_pos(s, _):
        pos[s] = jnp.where(s < total, rows_s[0, 0, s] * R + cols_s[0, 0, s], -1)
        return 0

    lax.fori_loop(0, S, set_pos, 0)

    def set_inv(p, _):
        slot = jnp.int32(S)
        for s in range(S):
            slot = jnp.where(pos[s] == p, jnp.int32(s), slot)
        inv[p] = slot
        return 0

    lax.fori_loop(0, C * R, set_inv, 0)

    for o in range(1, Ro):
        j = ((yo - o + Ro) % Ro) * 2 + k
        arrived(xs.at[j], fr.at[j])
        cp = remote(xs.at[j], xs.at[j], fs.at[Ro - 1 + o], fr.at[j], inner, c)
        cp.start()
        fcopies.append(cp)
    arrived(xs.at[inner], fr.at[inner])
    c_adj.wait()
    for o in range(1, Ro):
        j = ((yo - o + Ro) % Ro) * 2 + 1 - k
        arrived(xs.at[j], fr.at[j])

    tables = [sorted(range(Z), key=lambda d, zz=zz: (-abs(d - zz), d)) for zz in range(Z)]
    order = []
    for kk in range(Z):
        v = jnp.int32(tables[0][kk])
        for zz in range(1, Z):
            v = jnp.where(z == zz, jnp.int32(tables[zz][kk]), v)
        order.append(v)

    def pick(n):
        v = order[0]
        for kk in range(1, Z):
            v = jnp.where(n == kk, order[kk], v)
        return v

    def partial(i):
        row = jnp.concatenate([tiles[inv[i * R + j]] for j in range(R)], axis=1)
        return dot(row, xs[...].reshape(R * T, F))

    side = z + 1 - 2 * (z % 2)
    at_side = jnp.int32(0)
    for kk in range(Z):
        at_side = jnp.where(order[kk] == side, jnp.int32(kk), at_side)
    c_side = remote(xsend.at[at_side, Q - 1], xside, loc.at[10], loc.at[11], r, side * 2 + x)

    def over_x(n, q):
        return jnp.logical_not((n == at_side) & (q == Q - 1))

    def px(n, q):
        return remote(xsend.at[n, q], xrecv.at[n, q], ps.at[n, q], pr.at[n, q], r, xpeer)

    def fwd_peer(n, _):
        xsend[n] = partial(pick(n) * 2 + 1 - x).astype(BF16).reshape(Q, T // Q, F)

        @pl.when(n == 0)
        def _():
            for q in range(Q):
                px(0, q).start()

        return 0

    lax.fori_loop(0, Z, fwd_peer, 0)
    c_side.start()

    def pz(n, d, q):
        right = d > z
        way = jnp.where(right, 0, 1)
        nxt = jnp.where(right, z + 1, z - 1)
        return remote(zsend.at[n, q], zrecv.at[way, d, q], zs.at[n, q], zr.at[way, d, q], r,
                      nxt * 2 + x)

    def fwd_chain(n, _):
        d = pick(n)
        accf[...] = partial(d * 2 + x).reshape(Q, T // Q, F)

        def piece(q, _):
            @pl.when(over_x(n, q))
            def _():
                px(n, q).wait_send()

            @pl.when((n + 1 == Z - 1) & (q == Q - 1))
            def _():
                arrived(xside, loc.at[11])
                xsend[Z - 1, Q - 1] = (
                    xsend[Z - 1, Q - 1].astype(F32) + xside[...].astype(F32)).astype(BF16)

            @pl.when((n < Z - 1) & over_x(n + 1, q))
            def _():
                px(n + 1, q).start()

            @pl.when(over_x(n, q))
            def _():
                arrived(xrecv.at[n, q], pr.at[n, q])
                accf[q] += xrecv[n, q].astype(F32)

            @pl.when((d >= z) & (z > 0))
            def _():
                arrived(zrecv.at[0, d, q], zr.at[0, d, q])
                accf[q] += zrecv[0, d, q].astype(F32)

            @pl.when((d <= z) & (z < Z - 1))
            def _():
                arrived(zrecv.at[1, d, q], zr.at[1, d, q])
                accf[q] += zrecv[1, d, q].astype(F32)

            @pl.when(d != z)
            def _():
                zsend[n, q] = accf[q].astype(BF16)
                pz(n, d, q).start()

            return 0

        lax.fori_loop(0, Q, piece, 0)
        return 0

    lax.fori_loop(0, Z, fwd_chain, 0)

    c_w.wait()
    c_g.wait()
    agg = accf[...].reshape(T, F).astype(BF16)
    pre = dot(agg, wv[...])
    sig = jax.nn.sigmoid(pre)
    grad = (gv[...].astype(F32) * sig * (1.0 + pre * (1.0 - sig))).astype(BF16)
    mt[c] = lax.dot_general(
        wv[...], grad, (((1,), (1,)), ((), ())), preferred_element_type=F32
    ).astype(BF16).reshape(Q, F // Q, T)

    def to_z(n, s, q, way):
        i = s * 2 + x
        return remote(mt.at[i, q], mt.at[i, q], ms.at[way, n, q], mr.at[i, q], r,
                      (z + 1 - 2 * way) * 2 + x)

    def to_peer(n, s, q):
        i = s * 2 + x
        return remote(mt.at[i, q], mt.at[i, q], ms.at[2, n, q], mr.at[i, q], r, xpeer)

    def spread(n, s, q, act):
        @pl.when((s <= z) & (z < Z - 1))
        def _():
            act(to_z(n, s, q, 0))

        @pl.when((s >= z) & (z > 0))
        def _():
            act(to_z(n, s, q, 1))

        @pl.when((s != side) | (q != Q - 1))
        def _():
            act(to_peer(n, s, q))

    for q in range(Q):
        spread(0, z, q, lambda cp: cp.start())

    aggv[...] = agg
    gradv[...] = grad
    actv[...] = (pre * sig).astype(BF16)
    c_act = pltpu.make_async_copy(actv, act_out, loc.at[4])
    c_act.start()

    def to_row(o):
        to = (c + o) % C
        return remote(wterm.at[pl.ds(pl.multiple_of(to * H, H), H)], wr1.at[o], w1s.at[o],
                      w1r.at[o], r, to)

    def add_blocks(blocks, first):
        left = jnp.concatenate([mt[i].reshape(F, T) for i in blocks], axis=1)
        for j in range(R):
            right = jnp.concatenate([tiles[inv[i * R + j]] for i in blocks], axis=0)
            if first:
                bacc[j] = dot(left, right)
            else:
                bacc[j] += dot(left, right)

    c_back = remote(mt.at[xpeer, Q - 1], mt.at[xpeer, Q - 1], loc.at[12], mr.at[xpeer, Q - 1], r,
                    side * 2 + x)
    add_blocks([c], True)

    def bwd_step(m, _):
        s = pick(Z - 1 - m)
        zi = s * 2 + x
        for q in range(Q):
            arrived(mt.at[zi, q], mr.at[zi, q])
            spread(m, s, q, lambda cp: cp.start())
        xi = pick(Z - m) * 2 + 1 - x
        for q in range(Q):
            arrived(mt.at[xi, q], mr.at[xi, q])

        @pl.when(m == 1)
        def _():
            c_back.start()

        add_blocks([zi, xi], False)

        @pl.when(m == 1)
        def _():
            aggt = jnp.transpose(aggv[...].astype(F32)).astype(BF16)
            wterm[...] = dot(aggt, gradv[...]).astype(BF16)
            for o in range(1, C):
                to_row(o).start()

        @pl.when(m == Z - 1)
        def _():
            sel = wterm[pl.ds(pl.multiple_of(c * H, H), H), :].astype(F32)
            for o in range(1, C):
                arrived(wr1.at[o], w1r.at[o])
                sel += wr1[o].astype(F32)
            wr2[r] = sel.astype(BF16)
            for o in range(1, R):
                remote(wr2.at[r], wr2.at[r], w2s.at[o], w2r.at[r], (r + o) % R, c).start()

        return 0

    lax.fori_loop(1, Z, bwd_step, 0)
    xi = pick(0) * 2 + 1 - x
    for q in range(Q):
        arrived(mt.at[xi, q], mr.at[xi, q])
    add_blocks([xi], False)

    def bx(o):
        to = (yo + o) % Ro
        return remote(bsend.at[o], brecv.at[o], bs.at[o], br.at[o], r - r % 2 + 1 - k, c)

    for o in list(range(1, Ro)) + [0]:
        to = (yo + o) % Ro
        bsend[o] = bacc[to * 2 + 1 - k].astype(BF16)
        bx(o).start()
    bcopies = []
    for o in range(1, Ro):
        to = (yo + o) % Ro
        arrived(brecv.at[o], br.at[o])
        osend[o] = (bacc[to * 2 + k] + brecv[o].astype(F32)).astype(BF16)
        cp = remote(osend.at[o], orecv.at[o], os_.at[o], or_.at[o], to * 2 + k, c)
        cp.start()
        bcopies.append(cp)

    for o in range(1, R):
        arrived(wr2.at[(r + o) % R], w2r.at[(r + o) % R])
    sel = wr2[0].astype(F32)
    for j in range(1, R):
        sel += wr2[j].astype(F32)
    wr3[pl.ds(pl.multiple_of(c * H, H), H), :] = (sel * scale).astype(BF16)
    mine = wr3.at[pl.ds(pl.multiple_of(c * H, H), H)]
    w3copies = []
    for o in range(1, C):
        cp = remote(mine, mine, w3s.at[o], w3r.at[c], r, (c + o) % C)
        cp.start()
        w3copies.append(cp)

    arrived(brecv.at[0], br.at[0])
    xg = bacc[r] + brecv[0].astype(F32)
    for o in range(1, Ro):
        arrived(orecv.at[o], or_.at[o])
        xg += orecv[o].astype(F32)
    xgv[...] = jnp.transpose(xg).astype(BF16)
    c_xg = pltpu.make_async_copy(xgv, xg_out, loc.at[5])
    c_xg.start()

    for o in range(1, C):
        src = (c + o) % C
        arrived(wr3.at[pl.ds(pl.multiple_of(src * H, H), H)], w3r.at[src])
    wgv[...] = wr3[...].astype(F32)
    c_wg = pltpu.make_async_copy(wgv, wg_out, loc.at[6])
    c_wg.start()

    c_side.wait_send()
    c_back.wait_send()
    for cp in fcopies:
        cp.wait_send()

    def sent(n, _):
        d = pick(n)
        for q in range(Q):
            @pl.when(d != z)
            def _():
                pz(n, d, q).wait_send()

            spread(n, pick(Z - 1 - n), q, lambda cp: cp.wait_send())

        return 0

    lax.fori_loop(0, Z, sent, 0)
    for o in range(1, C):
        to_row(o).wait_send()
    for cp in w3copies + bcopies:
        cp.wait_send()
    for o in range(1, R):
        remote(wr2.at[r], wr2.at[r], w2s.at[o], w2r.at[r], (r + o) % R, c).wait_send()
    for o in range(Ro):
        bx(o).wait_send()
    c_act.wait()
    c_xg.wait()
    c_wg.wait()


def hand_out(*refs):
    held, sems = refs[6:9], refs[9]
    come = [pltpu.make_async_copy(refs[n], held[n], sems.at[n]) for n in range(3)]
    go = [pltpu.make_async_copy(held[n], refs[3 + n], sems.at[3 + n]) for n in range(3)]
    for cp in come:
        cp.start()
    for n in range(3):
        come[n].wait()
        go[n].start()
    for cp in go:
        cp.wait()


def local(features, adj_tiles, tile_rows, tile_cols, tile_count, weight, grad_out):
    R, C = lax.axis_size("row"), lax.axis_size("col")
    S, T = adj_tiles.shape[2], adj_tiles.shape[3]
    B, F = features.shape
    assert B == T and R % 2 == 0 and C % 4 == 0 and C >= 8 and T % (16 * C) == 0
    Ro, Z = R // 2, C // 2
    H = T // C
    hbm = pl.BlockSpec(memory_space=pltpu.HBM)
    any_space = pl.BlockSpec(memory_space=pl.ANY)
    V = pltpu.VMEM
    dma = pltpu.SemaphoreType.DMA
    outs = pl.pallas_call(
        functools.partial(kernel, R, C, S, T, F, 1.0 / math.sqrt(B * R * C)),
        out_shape=(
            jax.ShapeDtypeStruct((B, F), BF16),
            jax.ShapeDtypeStruct((F, F), F32),
            jax.ShapeDtypeStruct((B, F), BF16),
        ),
        in_specs=[hbm] * 7,
        out_specs=(any_space, any_space, any_space),
        scratch_shapes=[
            V((S + 1, T, T), BF16), V((R, T, F), BF16), V((F, F), BF16), V((T, F), BF16),
            pltpu.SMEM((1, 1, S), jnp.int32), pltpu.SMEM((1, 1, S), jnp.int32),
            pltpu.SMEM((1, 1), jnp.int32),
            pltpu.SMEM((S,), jnp.int32), pltpu.SMEM((C * R,), jnp.int32), V((Q, T // Q, F), F32),
            V((Z, Q, T // Q, F), BF16), V((Z, Q, T // Q, F), BF16), V((T // Q, F), BF16),
            V((Z, Q, T // Q, F), BF16),
            V((2, Z, Q, T // Q, F), BF16),
            V((T, F), BF16), V((T, F), BF16), V((T, F), BF16), V((C, Q, F // Q, T), BF16), V((R, F, T), F32),
            V((Ro, F, T), BF16), V((Ro, F, T), BF16), V((Ro, F, T), BF16), V((Ro, F, T), BF16),
            V((T, F), BF16),
            V((F, F), BF16), V((C, H, F), BF16), V((R, H, F), BF16), V((F, F), BF16),
            V((F, F), F32),
            dma((13,)), dma((2 * Ro,)), dma((R,)), dma((Z, Q)), dma((Z, Q)), dma((Z, Q)),
            dma((2, Z, Q)), dma((3, Z, Q)), dma((C, Q)), dma((Ro,)), dma((Ro,)), dma((Ro,)), dma((Ro,)),
            dma((C,)), dma((C,)), dma((R,)), dma((R,)), dma((C,)), dma((C,)),
        ],
        compiler_params=pltpu.CompilerParams(
            collective_id=0, has_side_effects=True, vmem_limit_bytes=62 * 1024 * 1024,
        ),
        cost_estimate=pl.CostEstimate(
            flops=4 * C * R * T * T * F, bytes_accessed=2 * S * T * T, transcendentals=T * F),
    )(features, adj_tiles, tile_rows, tile_cols, tile_count, weight, grad_out)
    return pl.pallas_call(
        hand_out,
        out_shape=tuple(jax.ShapeDtypeStruct(o.shape, o.dtype) for o in outs),
        in_specs=[any_space] * 3,
        out_specs=(hbm,) * 3,
        scratch_shapes=[V(o.shape, o.dtype) for o in outs] + [dma((6,))],
        compiler_params=pltpu.CompilerParams(vmem_limit_bytes=62 * 1024 * 1024),
    )(*outs)


def solution(mesh):
    return jax.shard_map(
        local,
        mesh=mesh,
        in_specs=(
            P(("col", "row"), None),
            P("row", "col", None, None, None),
            P("row", "col", None),
            P("row", "col", None),
            P("row", "col"),
            P(),
            P(("row", "col"), None),
        ),
        out_specs=(P(("row", "col"), None), P(), P(("col", "row"), None)),
        check_vma=False,
    )
```

```python
import functools
import math

import jax
import jax.numpy as jnp
from jax import lax
from jax.experimental import pallas as pl
from jax.experimental.pallas import tpu as pltpu
from jax.sharding import PartitionSpec as P

MESH = pl.DeviceIdType.MESH
BF16 = jnp.bfloat16
F32 = jnp.float32
Q = 2


def dot(a, b):
    return jnp.dot(a, b, preferred_element_type=F32)


def kernel(
    R, C, S, T, F, scale,
    feat, adj, trow, tcol, tcnt, wt, gout,
    act_out, wg_out, xg_out,
    tiles, xs, wv, gv, rows_s, cols_s, cnt_s, pos, inv, accf,
    xsend, xrecv, zsend, zrecv, actv, aggv, gradv, mt, bacc,
    bsend, brecv, osend, orecv, xgv,
    wterm, wr1, wr2, wr3, wgv,
    loc, fs, fr, ps, pr, zs, zr, ms, mr, bs, br, os_, or_,
    w1s, w1r, w2s, w2r, w3s, w3r,
):
    r = lax.axis_index("row")
    c = lax.axis_index("col")
    Ro, Z = R // 2, C // 2
    yo, k = r // 2, r % 2
    z, x = c // 2, c % 2
    inner = yo * 2 + 1 - k
    xpeer = z * 2 + 1 - x
    H = T // C

    def remote(src, dst, ss, rs, row, col):
        return pltpu.make_async_remote_copy(
            src_ref=src, dst_ref=dst, send_sem=ss, recv_sem=rs,
            device_id={"row": row, "col": col}, device_id_type=MESH,
        )

    def arrived(dst, rs):
        pltpu.make_async_copy(dst, dst, rs).wait()

    c_feat = pltpu.make_async_copy(feat, xs.at[r], loc.at[0])
    c_feat.start()
    c_adj = pltpu.make_async_copy(adj.at[0, 0], tiles.at[pl.ds(0, S)], loc.at[1])
    c_adj.start()
    c_w = pltpu.make_async_copy(wt, wv, loc.at[2])
    c_w.start()
    c_g = pltpu.make_async_copy(gout, gv, loc.at[3])
    c_g.start()

    c_ids = [
        pltpu.make_async_copy(src, dst, loc.at[7 + n])
        for n, (src, dst) in enumerate(((trow, rows_s), (tcol, cols_s), (tcnt, cnt_s)))
    ]
    for cp in c_ids:
        cp.start()

    barrier = pltpu.get_barrier_semaphore()
    for o in range(1, R):
        pl.semaphore_signal(
            barrier, inc=1, device_id={"row": (r + o) % R, "col": c}, device_id_type=MESH)
    for o in range(1, C):
        pl.semaphore_signal(
            barrier, inc=1, device_id={"row": r, "col": (c + o) % C}, device_id_type=MESH)
    pl.semaphore_wait(barrier, R - 1 + C - 1)

    c_feat.wait()
    fcopies = []

    def send_feat(j, q, sem, row):
        part = xs.at[j, pl.ds(q * (T // Q), T // Q)]
        cp = remote(part, part, fs.at[sem, q], fr.at[j, q], row, c)
        cp.start()
        fcopies.append(cp)

    def wait_feat(j, q):
        arrived(xs.at[j, pl.ds(q * (T // Q), T // Q)], fr.at[j, q])

    for q in range(Q):
        for o in range(1, Ro):
            send_feat(r, q, o, ((yo + o) % Ro) * 2 + k)
    for q in range(Q):
        send_feat(r, q, 0, inner)
    tiles[S] = jnp.zeros((T, T), BF16)
    for o in range(1, Ro):
        j = ((yo - o + Ro) % Ro) * 2 + k
        for q in range(Q):
            wait_feat(j, q)
            send_feat(j, q, Ro - 1 + o, inner)

    for cp in c_ids:
        cp.wait()
    total = cnt_s[0, 0]

    def set_pos(s, _):
        pos[s] = jnp.where(s < total, rows_s[0, 0, s] * R + cols_s[0, 0, s], -1)
        return 0

    lax.fori_loop(0, S, set_pos, 0)

    def set_inv(p, _):
        slot = jnp.int32(S)
        for s in range(S):
            slot = jnp.where(pos[s] == p, jnp.int32(s), slot)
        inv[p] = slot
        return 0

    lax.fori_loop(0, C * R, set_inv, 0)

    c_adj.wait()
    for q in range(Q):
        wait_feat(inner, q)
        for o in range(1, Ro):
            wait_feat(((yo - o + Ro) % Ro) * 2 + 1 - k, q)

    tables = [sorted(range(Z), key=lambda d, zz=zz: (-abs(d - zz), d)) for zz in range(Z)]
    order = []
    for kk in range(Z):
        v = jnp.int32(tables[0][kk])
        for zz in range(1, Z):
            v = jnp.where(z == zz, jnp.int32(tables[zz][kk]), v)
        order.append(v)

    def pick(n):
        v = order[0]
        for kk in range(1, Z):
            v = jnp.where(n == kk, order[kk], v)
        return v

    def partial(i):
        row = jnp.concatenate([tiles[inv[i * R + j]] for j in range(R)], axis=1)
        return dot(row, xs[...].reshape(R * T, F))

    def px(n, q):
        return remote(xsend.at[n, q], xrecv.at[n, q], ps.at[n, q], pr.at[n, q], r, xpeer)

    def fwd_peer(n, _):
        xsend[n] = partial(pick(n) * 2 + 1 - x).astype(BF16).reshape(Q, T // Q, F)

        @pl.when(n == 0)
        def _():
            for q in range(Q):
                px(0, q).start()

        return 0

    lax.fori_loop(0, Z, fwd_peer, 0)

    def pz(n, d, q):
        right = d > z
        way = jnp.where(right, 0, 1)
        nxt = jnp.where(right, z + 1, z - 1)
        return remote(zsend.at[n, q], zrecv.at[way, d, q], zs.at[n, q], zr.at[way, d, q], r,
                      nxt * 2 + x)

    def fwd_chain(n, _):
        d = pick(n)
        accf[...] = partial(d * 2 + x).reshape(Q, T // Q, F)

        def piece(q, _):
            px(n, q).wait_send()

            @pl.when(n < Z - 1)
            def _():
                px(n + 1, q).start()

            arrived(xrecv.at[n, q], pr.at[n, q])
            accf[q] += xrecv[n, q].astype(F32)

            @pl.when((d >= z) & (z > 0))
            def _():
                arrived(zrecv.at[0, d, q], zr.at[0, d, q])
                accf[q] += zrecv[0, d, q].astype(F32)

            @pl.when((d <= z) & (z < Z - 1))
            def _():
                arrived(zrecv.at[1, d, q], zr.at[1, d, q])
                accf[q] += zrecv[1, d, q].astype(F32)

            @pl.when(d != z)
            def _():
                zsend[n, q] = accf[q].astype(BF16)
                pz(n, d, q).start()

            return 0

        lax.fori_loop(0, Q, piece, 0)
        return 0

    lax.fori_loop(0, Z, fwd_chain, 0)

    c_w.wait()
    c_g.wait()
    agg = accf[...].reshape(T, F).astype(BF16)
    pre = dot(agg, wv[...])
    sig = jax.nn.sigmoid(pre)
    grad = (gv[...].astype(F32) * sig * (1.0 + pre * (1.0 - sig))).astype(BF16)
    mt[c] = lax.dot_general(
        wv[...], grad, (((1,), (1,)), ((), ())), preferred_element_type=F32
    ).astype(BF16).reshape(Q, F // Q, T)

    def to_z(n, s, q, way):
        i = s * 2 + x
        return remote(mt.at[i, q], mt.at[i, q], ms.at[way, n, q], mr.at[i, q], r,
                      (z + 1 - 2 * way) * 2 + x)

    def to_peer(n, s, q):
        i = s * 2 + x
        return remote(mt.at[i, q], mt.at[i, q], ms.at[2, n, q], mr.at[i, q], r, xpeer)

    def spread(n, s, q, act):
        @pl.when((s <= z) & (z < Z - 1))
        def _():
            act(to_z(n, s, q, 0))

        @pl.when((s >= z) & (z > 0))
        def _():
            act(to_z(n, s, q, 1))

        act(to_peer(n, s, q))

    for q in range(Q):
        spread(0, z, q, lambda cp: cp.start())

    aggv[...] = agg
    gradv[...] = grad
    actv[...] = (pre * sig).astype(BF16)
    c_act = pltpu.make_async_copy(actv, act_out, loc.at[4])
    c_act.start()

    def to_row(o):
        to = (c + o) % C
        return remote(wterm.at[pl.ds(pl.multiple_of(to * H, H), H)], wr1.at[o], w1s.at[o],
                      w1r.at[o], r, to)

    def add_blocks(blocks, first):
        left = jnp.concatenate([mt[i].reshape(F, T) for i in blocks], axis=1)
        for j in range(R):
            right = jnp.concatenate([tiles[inv[i * R + j]] for i in blocks], axis=0)
            if first:
                bacc[j] = dot(left, right)
            else:
                bacc[j] += dot(left, right)

    add_blocks([c], True)

    def bwd_step(m, _):
        s = pick(Z - 1 - m)
        zi = s * 2 + x
        for q in range(Q):
            arrived(mt.at[zi, q], mr.at[zi, q])
            spread(m, s, q, lambda cp: cp.start())
        xi = pick(Z - m) * 2 + 1 - x
        for q in range(Q):
            arrived(mt.at[xi, q], mr.at[xi, q])
        add_blocks([zi, xi], False)

        @pl.when(m == 1)
        def _():
            aggt = jnp.transpose(aggv[...].astype(F32)).astype(BF16)
            wterm[...] = dot(aggt, gradv[...]).astype(BF16)
            for o in range(1, C):
                to_row(o).start()

        @pl.when(m == Z - 1)
        def _():
            sel = wterm[pl.ds(pl.multiple_of(c * H, H), H), :].astype(F32)
            for o in range(1, C):
                arrived(wr1.at[o], w1r.at[o])
                sel += wr1[o].astype(F32)
            wr2[r] = sel.astype(BF16)
            for o in range(1, R):
                remote(wr2.at[r], wr2.at[r], w2s.at[o], w2r.at[r], (r + o) % R, c).start()

        return 0

    lax.fori_loop(1, Z, bwd_step, 0)
    xi = pick(0) * 2 + 1 - x
    for q in range(Q):
        arrived(mt.at[xi, q], mr.at[xi, q])
    add_blocks([xi], False)

    def bx(o):
        to = (yo + o) % Ro
        return remote(bsend.at[o], brecv.at[o], bs.at[o], br.at[o], r - r % 2 + 1 - k, c)

    for o in list(range(1, Ro)) + [0]:
        to = (yo + o) % Ro
        bsend[o] = bacc[to * 2 + 1 - k].astype(BF16)
        bx(o).start()
    bcopies = []
    for o in range(1, Ro):
        to = (yo + o) % Ro
        arrived(brecv.at[o], br.at[o])
        osend[o] = (bacc[to * 2 + k] + brecv[o].astype(F32)).astype(BF16)
        cp = remote(osend.at[o], orecv.at[o], os_.at[o], or_.at[o], to * 2 + k, c)
        cp.start()
        bcopies.append(cp)

    for o in range(1, R):
        arrived(wr2.at[(r + o) % R], w2r.at[(r + o) % R])
    sel = wr2[0].astype(F32)
    for j in range(1, R):
        sel += wr2[j].astype(F32)
    wr3[pl.ds(pl.multiple_of(c * H, H), H), :] = (sel * scale).astype(BF16)
    mine = wr3.at[pl.ds(pl.multiple_of(c * H, H), H)]
    w3copies = []
    for o in range(1, C):
        cp = remote(mine, mine, w3s.at[o], w3r.at[c], r, (c + o) % C)
        cp.start()
        w3copies.append(cp)

    arrived(brecv.at[0], br.at[0])
    xg = bacc[r] + brecv[0].astype(F32)
    for o in range(1, Ro):
        arrived(orecv.at[o], or_.at[o])
        xg += orecv[o].astype(F32)
    xgv[...] = jnp.transpose(xg).astype(BF16)
    c_xg = pltpu.make_async_copy(xgv, xg_out, loc.at[5])
    c_xg.start()

    for o in range(1, C):
        src = (c + o) % C
        arrived(wr3.at[pl.ds(pl.multiple_of(src * H, H), H)], w3r.at[src])
    wgv[...] = wr3[...].astype(F32)
    c_wg = pltpu.make_async_copy(wgv, wg_out, loc.at[6])
    c_wg.start()

    for cp in fcopies:
        cp.wait_send()

    def sent(n, _):
        d = pick(n)
        for q in range(Q):
            @pl.when(d != z)
            def _():
                pz(n, d, q).wait_send()

            spread(n, pick(Z - 1 - n), q, lambda cp: cp.wait_send())

        return 0

    lax.fori_loop(0, Z, sent, 0)
    for o in range(1, C):
        to_row(o).wait_send()
    for cp in w3copies + bcopies:
        cp.wait_send()
    for o in range(1, R):
        remote(wr2.at[r], wr2.at[r], w2s.at[o], w2r.at[r], (r + o) % R, c).wait_send()
    for o in range(Ro):
        bx(o).wait_send()
    c_act.wait()
    c_xg.wait()
    c_wg.wait()


def hand_out(*refs):
    held, sems = refs[6:9], refs[9]
    come = [pltpu.make_async_copy(refs[n], held[n], sems.at[n]) for n in range(3)]
    go = [pltpu.make_async_copy(held[n], refs[3 + n], sems.at[3 + n]) for n in range(3)]
    for cp in come:
        cp.start()
    for n in range(3):
        come[n].wait()
        go[n].start()
    for cp in go:
        cp.wait()


def local(features, adj_tiles, tile_rows, tile_cols, tile_count, weight, grad_out):
    R, C = lax.axis_size("row"), lax.axis_size("col")
    S, T = adj_tiles.shape[2], adj_tiles.shape[3]
    B, F = features.shape
    assert B == T and R % 2 == 0 and C % 2 == 0 and T % (16 * C) == 0
    Ro, Z = R // 2, C // 2
    H = T // C
    hbm = pl.BlockSpec(memory_space=pltpu.HBM)
    any_space = pl.BlockSpec(memory_space=pl.ANY)
    V = pltpu.VMEM
    dma = pltpu.SemaphoreType.DMA
    outs = pl.pallas_call(
        functools.partial(kernel, R, C, S, T, F, 1.0 / math.sqrt(B * R * C)),
        out_shape=(
            jax.ShapeDtypeStruct((B, F), BF16),
            jax.ShapeDtypeStruct((F, F), F32),
            jax.ShapeDtypeStruct((B, F), BF16),
        ),
        in_specs=[hbm] * 7,
        out_specs=(any_space, any_space, any_space),
        scratch_shapes=[
            V((S + 1, T, T), BF16), V((R, T, F), BF16), V((F, F), BF16), V((T, F), BF16),
            pltpu.SMEM((1, 1, S), jnp.int32), pltpu.SMEM((1, 1, S), jnp.int32),
            pltpu.SMEM((1, 1), jnp.int32),
            pltpu.SMEM((S,), jnp.int32), pltpu.SMEM((C * R,), jnp.int32), V((Q, T // Q, F), F32),
            V((Z, Q, T // Q, F), BF16), V((Z, Q, T // Q, F), BF16), V((Z, Q, T // Q, F), BF16),
            V((2, Z, Q, T // Q, F), BF16),
            V((T, F), BF16), V((T, F), BF16), V((T, F), BF16), V((C, Q, F // Q, T), BF16), V((R, F, T), F32),
            V((Ro, F, T), BF16), V((Ro, F, T), BF16), V((Ro, F, T), BF16), V((Ro, F, T), BF16),
            V((T, F), BF16),
            V((F, F), BF16), V((C, H, F), BF16), V((R, H, F), BF16), V((F, F), BF16),
            V((F, F), F32),
            dma((10,)), dma((2 * Ro, Q)), dma((R, Q)), dma((Z, Q)), dma((Z, Q)), dma((Z, Q)),
            dma((2, Z, Q)), dma((3, Z, Q)), dma((C, Q)), dma((Ro,)), dma((Ro,)), dma((Ro,)), dma((Ro,)),
            dma((C,)), dma((C,)), dma((R,)), dma((R,)), dma((C,)), dma((C,)),
        ],
        compiler_params=pltpu.CompilerParams(
            collective_id=0, has_side_effects=True, vmem_limit_bytes=62 * 1024 * 1024,
        ),
        cost_estimate=pl.CostEstimate(
            flops=4 * C * R * T * T * F, bytes_accessed=2 * S * T * T, transcendentals=T * F),
    )(features, adj_tiles, tile_rows, tile_cols, tile_count, weight, grad_out)
    return pl.pallas_call(
        hand_out,
        out_shape=tuple(jax.ShapeDtypeStruct(o.shape, o.dtype) for o in outs),
        in_specs=[any_space] * 3,
        out_specs=(hbm,) * 3,
        scratch_shapes=[V(o.shape, o.dtype) for o in outs] + [dma((6,))],
        compiler_params=pltpu.CompilerParams(vmem_limit_bytes=62 * 1024 * 1024),
    )(*outs)


def solution(mesh):
    return jax.shard_map(
        local,
        mesh=mesh,
        in_specs=(
            P(("col", "row"), None),
            P("row", "col", None, None, None),
            P("row", "col", None),
            P("row", "col", None),
            P("row", "col"),
            P(),
            P(("row", "col"), None),
        ),
        out_specs=(P(("row", "col"), None), P(), P(("col", "row"), None)),
        check_vma=False,
    )
```

```python
import functools
import math

import jax
import jax.numpy as jnp
from jax import lax
from jax.experimental import pallas as pl
from jax.experimental.pallas import tpu as pltpu
from jax.sharding import PartitionSpec as P

MESH = pl.DeviceIdType.MESH
BF16 = jnp.bfloat16
F32 = jnp.float32
Q = 2


def dot(a, b):
    return jnp.dot(a, b, preferred_element_type=F32)


def kernel(
    R, C, S, T, F, scale,
    feat, adj, trow, tcol, tcnt, wt, gout,
    act_out, wg_out, xg_out,
    tiles, xs, wv, gv, rows_s, cols_s, cnt_s, pos, inv, accf,
    xsend, xrecv, zsend, zrecv, actv, aggv, gradv, mt, bacc,
    bsend, brecv, osend, orecv, xgv,
    wterm, wr1, wr2, wr3, wgv,
    loc, fs, fr, ps, pr, zs, zr, ms, mr, bs, br, os_, or_,
    w1s, w1r, w2s, w2r, w3s, w3r,
):
    r = lax.axis_index("row")
    c = lax.axis_index("col")
    Ro, Z = R // 2, C // 2
    yo, k = r // 2, r % 2
    z, x = c // 2, c % 2
    inner = yo * 2 + 1 - k
    xpeer = z * 2 + 1 - x
    H = T // C

    def remote(src, dst, ss, rs, row, col):
        return pltpu.make_async_remote_copy(
            src_ref=src, dst_ref=dst, send_sem=ss, recv_sem=rs,
            device_id={"row": row, "col": col}, device_id_type=MESH,
        )

    def arrived(dst, rs):
        pltpu.make_async_copy(dst, dst, rs).wait()

    c_feat = pltpu.make_async_copy(feat, xs.at[r], loc.at[0])
    c_feat.start()
    c_adj = pltpu.make_async_copy(adj.at[0, 0], tiles.at[pl.ds(0, S)], loc.at[1])
    c_adj.start()
    c_w = pltpu.make_async_copy(wt, wv, loc.at[2])
    c_w.start()
    c_g = pltpu.make_async_copy(gout, gv, loc.at[3])
    c_g.start()

    c_ids = [
        pltpu.make_async_copy(src, dst, loc.at[7 + n])
        for n, (src, dst) in enumerate(((trow, rows_s), (tcol, cols_s), (tcnt, cnt_s)))
    ]
    for cp in c_ids:
        cp.start()

    barrier = pltpu.get_barrier_semaphore()
    for o in range(1, R):
        pl.semaphore_signal(
            barrier, inc=1, device_id={"row": (r + o) % R, "col": c}, device_id_type=MESH)
    for o in range(1, C):
        pl.semaphore_signal(
            barrier, inc=1, device_id={"row": r, "col": (c + o) % C}, device_id_type=MESH)
    pl.semaphore_wait(barrier, R - 1 + C - 1)

    c_feat.wait()
    fcopies = []
    for o in range(1, Ro):
        cp = remote(xs.at[r], xs.at[r], fs.at[o], fr.at[r], ((yo + o) % Ro) * 2 + k, c)
        cp.start()
        fcopies.append(cp)
    cp = remote(xs.at[r], xs.at[r], fs.at[0], fr.at[r], inner, c)
    cp.start()
    fcopies.append(cp)

    tiles[S] = jnp.zeros((T, T), BF16)
    for cp in c_ids:
        cp.wait()
    total = cnt_s[0, 0]

    def set_pos(s, _):
        pos[s] = jnp.where(s < total, rows_s[0, 0, s] * R + cols_s[0, 0, s], -1)
        return 0

    lax.fori_loop(0, S, set_pos, 0)

    def set_inv(step, _):
        slots = [jnp.int32(S)] * 8
        for s in range(S):
            held = pos[s] - step * 8
            slots = [jnp.where(held == u, jnp.int32(s), slots[u]) for u in range(8)]
        for u in range(8):
            inv[step * 8 + u] = slots[u]
        return 0

    lax.fori_loop(0, C * R // 8, set_inv, 0)

    for o in range(1, Ro):
        j = ((yo - o + Ro) % Ro) * 2 + k
        arrived(xs.at[j], fr.at[j])
        cp = remote(xs.at[j], xs.at[j], fs.at[Ro - 1 + o], fr.at[j], inner, c)
        cp.start()
        fcopies.append(cp)
    arrived(xs.at[inner], fr.at[inner])
    c_adj.wait()
    for o in range(1, Ro):
        j = ((yo - o + Ro) % Ro) * 2 + 1 - k
        arrived(xs.at[j], fr.at[j])

    tables = [sorted(range(Z), key=lambda d, zz=zz: (-abs(d - zz), d)) for zz in range(Z)]
    order = []
    for kk in range(Z):
        v = jnp.int32(tables[0][kk])
        for zz in range(1, Z):
            v = jnp.where(z == zz, jnp.int32(tables[zz][kk]), v)
        order.append(v)

    def pick(n):
        v = order[0]
        for kk in range(1, Z):
            v = jnp.where(n == kk, order[kk], v)
        return v

    def partial(i):
        row = jnp.concatenate([tiles[inv[i * R + j]] for j in range(R)], axis=1)
        return dot(row, xs[...].reshape(R * T, F))

    def px(n, q):
        return remote(xsend.at[n, q], xrecv.at[n, q], ps.at[n, q], pr.at[n, q], r, xpeer)

    def fwd_peer(n, _):
        xsend[n] = partial(pick(n) * 2 + 1 - x).astype(BF16).reshape(Q, T // Q, F)

        @pl.when(n == 0)
        def _():
            for q in range(Q):
                px(0, q).start()

        return 0

    lax.fori_loop(0, Z, fwd_peer, 0)

    def pz(n, d, q):
        right = d > z
        way = jnp.where(right, 0, 1)
        nxt = jnp.where(right, z + 1, z - 1)
        return remote(zsend.at[n, q], zrecv.at[way, d, q], zs.at[n, q], zr.at[way, d, q], r,
                      nxt * 2 + x)

    def fwd_chain(n, _):
        d = pick(n)
        accf[...] = partial(d * 2 + x).reshape(Q, T // Q, F)

        def piece(q, _):
            px(n, q).wait_send()

            @pl.when(n < Z - 1)
            def _():
                px(n + 1, q).start()

            arrived(xrecv.at[n, q], pr.at[n, q])
            accf[q] += xrecv[n, q].astype(F32)

            @pl.when((d >= z) & (z > 0))
            def _():
                arrived(zrecv.at[0, d, q], zr.at[0, d, q])
                accf[q] += zrecv[0, d, q].astype(F32)

            @pl.when((d <= z) & (z < Z - 1))
            def _():
                arrived(zrecv.at[1, d, q], zr.at[1, d, q])
                accf[q] += zrecv[1, d, q].astype(F32)

            @pl.when(d != z)
            def _():
                zsend[n, q] = accf[q].astype(BF16)
                pz(n, d, q).start()

            return 0

        lax.fori_loop(0, Q, piece, 0)
        return 0

    lax.fori_loop(0, Z, fwd_chain, 0)

    c_w.wait()
    c_g.wait()
    agg = accf[...].reshape(T, F).astype(BF16)
    pre = dot(agg, wv[...])
    sig = jax.nn.sigmoid(pre)
    grad = (gv[...].astype(F32) * sig * (1.0 + pre * (1.0 - sig))).astype(BF16)
    mt[c] = lax.dot_general(
        wv[...], grad, (((1,), (1,)), ((), ())), preferred_element_type=F32
    ).astype(BF16).reshape(Q, F // Q, T)

    def to_z(n, s, q, way):
        i = s * 2 + x
        return remote(mt.at[i, q], mt.at[i, q], ms.at[way, n, q], mr.at[i, q], r,
                      (z + 1 - 2 * way) * 2 + x)

    def to_peer(n, s, q):
        i = s * 2 + x
        return remote(mt.at[i, q], mt.at[i, q], ms.at[2, n, q], mr.at[i, q], r, xpeer)

    def spread(n, s, q, act):
        @pl.when((s <= z) & (z < Z - 1))
        def _():
            act(to_z(n, s, q, 0))

        @pl.when((s >= z) & (z > 0))
        def _():
            act(to_z(n, s, q, 1))

        act(to_peer(n, s, q))

    for q in range(Q):
        spread(0, z, q, lambda cp: cp.start())

    aggv[...] = agg
    gradv[...] = grad
    actv[...] = (pre * sig).astype(BF16)
    c_act = pltpu.make_async_copy(actv, act_out, loc.at[4])
    c_act.start()

    def to_row(o):
        to = (c + o) % C
        return remote(wterm.at[pl.ds(pl.multiple_of(to * H, H), H)], wr1.at[o], w1s.at[o],
                      w1r.at[o], r, to)

    def add_blocks(blocks, first):
        left = jnp.concatenate([mt[i].reshape(F, T) for i in blocks], axis=1)
        for j in range(R):
            right = jnp.concatenate([tiles[inv[i * R + j]] for i in blocks], axis=0)
            if first:
                bacc[j] = dot(left, right)
            else:
                bacc[j] += dot(left, right)

    add_blocks([c], True)

    def bwd_step(m, _):
        s = pick(Z - 1 - m)
        zi = s * 2 + x
        for q in range(Q):
            arrived(mt.at[zi, q], mr.at[zi, q])
            spread(m, s, q, lambda cp: cp.start())
        xi = pick(Z - m) * 2 + 1 - x
        for q in range(Q):
            arrived(mt.at[xi, q], mr.at[xi, q])
        add_blocks([zi, xi], False)

        @pl.when(m == 1)
        def _():
            aggt = jnp.transpose(aggv[...].astype(F32)).astype(BF16)
            wterm[...] = dot(aggt, gradv[...]).astype(BF16)
            for o in range(1, C):
                to_row(o).start()

        @pl.when(m == Z - 1)
        def _():
            sel = wterm[pl.ds(pl.multiple_of(c * H, H), H), :].astype(F32)
            for o in range(1, C):
                arrived(wr1.at[o], w1r.at[o])
                sel += wr1[o].astype(F32)
            wr2[r] = sel.astype(BF16)
            for o in range(1, R):
                remote(wr2.at[r], wr2.at[r], w2s.at[o], w2r.at[r], (r + o) % R, c).start()

        return 0

    lax.fori_loop(1, Z, bwd_step, 0)
    xi = pick(0) * 2 + 1 - x
    for q in range(Q):
        arrived(mt.at[xi, q], mr.at[xi, q])
    add_blocks([xi], False)

    def bx(o):
        to = (yo + o) % Ro
        return remote(bsend.at[o], brecv.at[o], bs.at[o], br.at[o], r - r % 2 + 1 - k, c)

    for o in list(range(1, Ro)) + [0]:
        to = (yo + o) % Ro
        bsend[o] = bacc[to * 2 + 1 - k].astype(BF16)
        bx(o).start()
    bcopies = []
    for o in range(1, Ro):
        to = (yo + o) % Ro
        arrived(brecv.at[o], br.at[o])
        osend[o] = (bacc[to * 2 + k] + brecv[o].astype(F32)).astype(BF16)
        cp = remote(osend.at[o], orecv.at[o], os_.at[o], or_.at[o], to * 2 + k, c)
        cp.start()
        bcopies.append(cp)

    for o in range(1, R):
        arrived(wr2.at[(r + o) % R], w2r.at[(r + o) % R])
    sel = wr2[0].astype(F32)
    for j in range(1, R):
        sel += wr2[j].astype(F32)
    wr3[pl.ds(pl.multiple_of(c * H, H), H), :] = (sel * scale).astype(BF16)
    mine = wr3.at[pl.ds(pl.multiple_of(c * H, H), H)]
    w3copies = []
    for o in range(1, C):
        cp = remote(mine, mine, w3s.at[o], w3r.at[c], r, (c + o) % C)
        cp.start()
        w3copies.append(cp)

    arrived(brecv.at[0], br.at[0])
    xg = bacc[r] + brecv[0].astype(F32)
    for o in range(1, Ro):
        arrived(orecv.at[o], or_.at[o])
        xg += orecv[o].astype(F32)
    xgv[...] = jnp.transpose(xg).astype(BF16)
    c_xg = pltpu.make_async_copy(xgv, xg_out, loc.at[5])
    c_xg.start()

    for o in range(1, C):
        src = (c + o) % C
        arrived(wr3.at[pl.ds(pl.multiple_of(src * H, H), H)], w3r.at[src])
    wgv[...] = wr3[...].astype(F32)
    c_wg = pltpu.make_async_copy(wgv, wg_out, loc.at[6])
    c_wg.start()

    for cp in fcopies:
        cp.wait_send()

    def sent(n, _):
        d = pick(n)
        for q in range(Q):
            @pl.when(d != z)
            def _():
                pz(n, d, q).wait_send()

            spread(n, pick(Z - 1 - n), q, lambda cp: cp.wait_send())

        return 0

    lax.fori_loop(0, Z, sent, 0)
    for o in range(1, C):
        to_row(o).wait_send()
    for cp in w3copies + bcopies:
        cp.wait_send()
    for o in range(1, R):
        remote(wr2.at[r], wr2.at[r], w2s.at[o], w2r.at[r], (r + o) % R, c).wait_send()
    for o in range(Ro):
        bx(o).wait_send()
    c_act.wait()
    c_xg.wait()
    c_wg.wait()


def hand_out(*refs):
    held, sems = refs[6:9], refs[9]
    come = [pltpu.make_async_copy(refs[n], held[n], sems.at[n]) for n in range(3)]
    go = [pltpu.make_async_copy(held[n], refs[3 + n], sems.at[3 + n]) for n in range(3)]
    for cp in come:
        cp.start()
    for n in range(3):
        come[n].wait()
        go[n].start()
    for cp in go:
        cp.wait()


def local(features, adj_tiles, tile_rows, tile_cols, tile_count, weight, grad_out):
    R, C = lax.axis_size("row"), lax.axis_size("col")
    S, T = adj_tiles.shape[2], adj_tiles.shape[3]
    B, F = features.shape
    assert B == T and R % 2 == 0 and C % 2 == 0 and T % (16 * C) == 0 and C * R % 8 == 0
    Ro, Z = R // 2, C // 2
    H = T // C
    hbm = pl.BlockSpec(memory_space=pltpu.HBM)
    any_space = pl.BlockSpec(memory_space=pl.ANY)
    V = pltpu.VMEM
    dma = pltpu.SemaphoreType.DMA
    outs = pl.pallas_call(
        functools.partial(kernel, R, C, S, T, F, 1.0 / math.sqrt(B * R * C)),
        out_shape=(
            jax.ShapeDtypeStruct((B, F), BF16),
            jax.ShapeDtypeStruct((F, F), F32),
            jax.ShapeDtypeStruct((B, F), BF16),
        ),
        in_specs=[hbm] * 7,
        out_specs=(any_space, any_space, any_space),
        scratch_shapes=[
            V((S + 1, T, T), BF16), V((R, T, F), BF16), V((F, F), BF16), V((T, F), BF16),
            pltpu.SMEM((1, 1, S), jnp.int32), pltpu.SMEM((1, 1, S), jnp.int32),
            pltpu.SMEM((1, 1), jnp.int32),
            pltpu.SMEM((S,), jnp.int32), pltpu.SMEM((C * R,), jnp.int32), V((Q, T // Q, F), F32),
            V((Z, Q, T // Q, F), BF16), V((Z, Q, T // Q, F), BF16), V((Z, Q, T // Q, F), BF16),
            V((2, Z, Q, T // Q, F), BF16),
            V((T, F), BF16), V((T, F), BF16), V((T, F), BF16), V((C, Q, F // Q, T), BF16), V((R, F, T), F32),
            V((Ro, F, T), BF16), V((Ro, F, T), BF16), V((Ro, F, T), BF16), V((Ro, F, T), BF16),
            V((T, F), BF16),
            V((F, F), BF16), V((C, H, F), BF16), V((R, H, F), BF16), V((F, F), BF16),
            V((F, F), F32),
            dma((10,)), dma((2 * Ro,)), dma((R,)), dma((Z, Q)), dma((Z, Q)), dma((Z, Q)),
            dma((2, Z, Q)), dma((3, Z, Q)), dma((C, Q)), dma((Ro,)), dma((Ro,)), dma((Ro,)), dma((Ro,)),
            dma((C,)), dma((C,)), dma((R,)), dma((R,)), dma((C,)), dma((C,)),
        ],
        compiler_params=pltpu.CompilerParams(
            collective_id=0, has_side_effects=True, vmem_limit_bytes=62 * 1024 * 1024,
        ),
        cost_estimate=pl.CostEstimate(
            flops=4 * C * R * T * T * F, bytes_accessed=2 * S * T * T, transcendentals=T * F),
    )(features, adj_tiles, tile_rows, tile_cols, tile_count, weight, grad_out)
    return pl.pallas_call(
        hand_out,
        out_shape=tuple(jax.ShapeDtypeStruct(o.shape, o.dtype) for o in outs),
        in_specs=[any_space] * 3,
        out_specs=(hbm,) * 3,
        scratch_shapes=[V(o.shape, o.dtype) for o in outs] + [dma((6,))],
        compiler_params=pltpu.CompilerParams(vmem_limit_bytes=62 * 1024 * 1024),
    )(*outs)


def solution(mesh):
    return jax.shard_map(
        local,
        mesh=mesh,
        in_specs=(
            P(("col", "row"), None),
            P("row", "col", None, None, None),
            P("row", "col", None),
            P("row", "col", None),
            P("row", "col"),
            P(),
            P(("row", "col"), None),
        ),
        out_specs=(P(("row", "col"), None), P(), P(("col", "row"), None)),
        check_vma=False,
    )
```
